32 devices in a mesh: grid: 8 (over y, x, core), band: 4 (over z).
Axes of the slice: x: 2, y: 2, z: 4, core: 2. Of those that a mesh axis runs over, the one named last changes fastest.
Arguments:
- residual: float32 [32, 64, 32, 384], P('band', 'grid')
- direction: float32 [32, 64, 32, 384], P('band', 'grid'), may hold values from -2 to 2
- solution: float32 [32, 64, 32, 384], P('band', 'grid'), may hold values from -6 to 6
- old_product: float32 [32], P('band'), may hold values from 157286.4 to 629145.6
- orbitals: bfloat16 [32, 64, 32, 384], P('band', 'grid')
- energies: float32 [32], replicated, may hold values from -3 to -0.3
- potential: float32 [64, 32, 384], P('grid'), may hold values from 0.5 to 3
- column_index: int32 [32], P('band'), may hold values from 0 to 95
- panel_index: int32 [32], P('band'), may hold values from 0 to 1
Outputs:
- new_solution: float32 [32, 64, 32, 384], P('band', 'grid')
- new_residual: float32 [32, 64, 32, 384], P('band', 'grid')
- new_direction: float32 [32, 64, 32, 384], P('band', 'grid')
- new_product: float32 [32], P('band')
The draws below stay inside these ranges and needn't reach their ends.
All inputs are finite; a program needn't handle non-finite values.
Results may differ from the reference program's by a relative error of at most 0.00085.
Values may be sent and summed in bfloat16 or wider, within the bound.
No kernel may reach another device: no remote copies, remote signals or barrier semaphores. Data moves between devices by JAX's collectives and lax.ppermute only.
A program may use at most 128 MiB of HBM per device.

```python
import math
import jax
import jax.numpy as jnp
from jax import lax

NY = 32
NZ = 384
PB = 16
PANELS = 2
NBANDS = 32
NCOLS = 96
C = 32
NX = 64


def shared_orbitals(key):
    return jax.random.normal(key, (NBANDS, NX, NY, NZ), jnp.float32)


def draw_orbitals(key, part):
    base = shared_orbitals(key)
    return base.astype(jnp.bfloat16)


def draw_residual(key, part):
    base = shared_orbitals(key)
    key = jax.random.fold_in(key, 23)
    weight_key, noise_key = jax.random.split(key)
    weights = 0.4 * jax.random.normal(weight_key, (C, NBANDS), jnp.float32)
    noise = jax.random.normal(noise_key, (C, NX, NY, NZ), jnp.float32)
    mixed = jnp.einsum('cb,bxyz->cxyz', weights, base, precision=lax.Precision.HIGHEST)
    return (noise + mixed).astype(jnp.float32)


def with_ends(array, rng, least, largest):
    dims = array.shape
    spot = [jax.random.randint(jax.random.fold_in(rng, axis), (), 0, dims[axis]) for axis in range(len(dims))]
    array = array.at[tuple(spot)].set(least)
    longest = dims.index(max(dims))
    spot[longest] = (spot[longest] + 1) % dims[longest]
    return array.at[tuple(spot)].set(largest)


def steps_of(key, extent, cuts, least, high):
    loudness, own = 1.0, jax.random.fold_in(key, 6)
    for dim, shards_of in cuts:
        draws = jnp.exp(jax.random.uniform(jax.random.fold_in(own, dim), (shards_of,), jnp.float32, least / len(cuts), high / len(cuts)))
        loudness = loudness * jnp.repeat(draws, extent[dim] // shards_of).reshape([-1 if axis == dim else 1 for axis in range(len(extent))])
    return loudness


def gaussian(stream_key, dims, width, limit, cuts=(), kind=jnp.bfloat16):
    result = width * jax.random.normal(stream_key, dims, jnp.float32)
    if cuts:
        result = result * steps_of(stream_key, dims, cuts, -0.22, 0.18)
    return jnp.clip(result, -limit, limit).astype(kind)


def setup_inputs(seed: int = 0) -> dict:
    splits = jax.random.split(jax.random.key(seed), 10)
    residual = draw_residual(jax.random.fold_in(splits[9], 71), 0)
    direction = gaussian(splits[1], (C, NX, NY, NZ), 0.3, 2.0, ((0, 4), (1, 8)), jnp.float32)
    solution = gaussian(splits[2], (C, NX, NY, NZ), 1.0, 6.0, ((0, 4), (1, 8)), jnp.float32)
    old_product = jnp.clip(jnp.exp(math.log(629145.6) - 1.3862944 * jax.random.uniform(splits[3], (C,), jnp.float32) ** steps_of(splits[3], (C,), ((0, 4),), -0.2, 0.2)), 157286.4, 629145.6)
    orbitals = draw_orbitals(jax.random.fold_in(splits[9], 71), 0)
    energies = jnp.clip(jax.random.uniform(splits[5], (NBANDS,), jnp.float32, -3.0, -0.3), -3.0, -0.3)
    potential = jnp.clip(0.5 + 2.5 * jax.random.uniform(splits[6], (NX, NY, NZ), jnp.float32) ** steps_of(splits[6], (NX, NY, NZ), ((0, 8),), -0.2, 0.2), 0.5, 3.0)
    column_index = with_ends(jax.random.randint(splits[7], (C,), 0, NCOLS), jax.random.fold_in(splits[7], 1), 0, NCOLS - 1).astype(jnp.int32)
    panel_index = with_ends(jax.random.randint(splits[8], (C,), 0, PANELS), jax.random.fold_in(splits[8], 1), 0, PANELS - 1).astype(jnp.int32)
    return {"residual": residual, "direction": direction, "solution": solution, "old_product": old_product, "orbitals": orbitals, "energies": energies, "potential": potential, "column_index": column_index, "panel_index": panel_index}


COEFFS = (-49.0 / 18.0, 3.0 / 2.0, -3.0 / 20.0, 1.0 / 90.0)


def operator_three(column, shifted):
    padded = jnp.pad(column, 3)
    extent_x, extent_y, extent_z = column.shape
    summed = 3.0 * COEFFS[0] * column
    for offset in range(1, 4):
        beside_all = padded[3 + offset:3 + offset + extent_x, 3:3 + extent_y, 3:3 + extent_z] + padded[3 - offset:3 - offset + extent_x, 3:3 + extent_y, 3:3 + extent_z]
        beside_all = beside_all + padded[3:3 + extent_x, 3 + offset:3 + offset + extent_y, 3:3 + extent_z] + padded[3:3 + extent_x, 3 - offset:3 - offset + extent_y, 3:3 + extent_z]
        beside_all = beside_all + padded[3:3 + extent_x, 3:3 + extent_y, 3 + offset:3 + offset + extent_z] + padded[3:3 + extent_x, 3:3 + extent_y, 3 - offset:3 - offset + extent_z]
        summed = summed + COEFFS[offset] * beside_all
    return -0.5 * summed + shifted * column


def reference(residual, direction, solution, old_product, orbitals, energies, potential, column_index, panel_index):
    wave = orbitals.astype(jnp.float32)
    cells = float(NX * NY * NZ)
    band_ids = jnp.arange(NBANDS, dtype=jnp.int32)

    def one_column(items):
        res_col, dir_col, sol_col, old_col, col_id, panel_id = items
        energy = jnp.sum(jnp.where(band_ids == col_id // 3, energies, jnp.float32(0.0)))
        shifted = potential - energy
        precond = shifted - 1.5 * COEFFS[0]
        start = res_col / precond
        correlation = jnp.einsum('xyz,bxyz->b', start, wave, precision=lax.Precision.HIGHEST)
        chosen = jnp.where(band_ids // PB == panel_id, correlation, jnp.float32(0.0)) / cells
        projected = start - jnp.einsum('b,bxyz->xyz', chosen, wave, precision=lax.Precision.HIGHEST)
        rr_now = jnp.sum(res_col * projected)
        new_dir = projected + (rr_now / old_col) * dir_col
        image = operator_three(new_dir, shifted)
        curvature = jnp.sum(new_dir * image)
        step_size = rr_now / curvature
        return sol_col + step_size * new_dir, res_col - step_size * image, new_dir, rr_now

    outputs = lax.map(one_column, (residual, direction, solution, old_product, column_index, panel_index))
    return (outputs[0], outputs[1], outputs[2], outputs[3])
```

```python
import functools

import jax
import jax.numpy as jnp
from jax import lax
from jax.experimental import pallas as pl
from jax.experimental.pallas import tpu as pltpu
from jax.sharding import PartitionSpec as P

PB = 16
K0 = -49.0 / 18.0
SIDE = (270.0, -27.0, 2.0)
SCALE = -0.5 / 180.0
F32, BF16 = jnp.float32, jnp.bfloat16
TILE = 16
MIB = 1 << 20
TOP = 16384.0
NT = (((1,), (1,)), ((), ()))
LANE_S, LANE_R, LANE_RS, LANE_CAP = 0, 32, 96, 100


def edge_plane(i):
    return i + 2 * (i // 3)


def high_plane(i):
    return i + 5


def mid_plane(i):
    return i + 3


def same_plane(i):
    return i


def plane_spec(shape, place, part=0):
    return pl.BlockSpec((shape[0], 1) + tuple(shape[2:]), lambda i: (part, place(i), 0, 0))


def piece(array, size, part, first=0):
    return array, (size,) + tuple(array.shape[1:]), part, first


def as_piece(x):
    return x if isinstance(x, tuple) else piece(x, x.shape[0], 0)


def piece_spec(x, planes, place):
    array, shape, part, first = x
    return plane_spec(shape, place if shape[1] == planes else (lambda i: i + first), part)


def whole_spec(shape):
    return pl.BlockSpec(tuple(shape), lambda i: (0,) * len(shape))


def params(limit):
    return pltpu.CompilerParams(vmem_limit_bytes=limit * MIB)


CHEAP = pl.CostEstimate(flops=10**6, bytes_accessed=MIB, transcendentals=0)


DIRECT = pl.BlockSpec(memory_space=pltpu.VMEM)


def near(shape, dtype):
    return pltpu.VMEM(tuple(shape), dtype)


def far(x):
    return pltpu.with_memory_space_constraint(x, pltpu.HBM)


def held(x):
    return pltpu.with_memory_space_constraint(x, pltpu.VMEM)


def dot(a, b):
    return jnp.dot(a, b, preferred_element_type=F32)


def exact_dot(a, b):
    return jnp.dot(a, b, precision=lax.Precision.HIGHEST, preferred_element_type=F32)


def split(x):
    high = x.astype(BF16)
    return high, (x - high.astype(F32)).astype(BF16)


def in_lane(column, lane):
    at = lax.broadcasted_iota(jnp.int32, (column.shape[0], 128), 1)
    return jnp.where(at == lane, column, 0.0)


def prepare_kernel(planes, r_ref, d_ref, v_ref, e_ref, o_ref, s_ref, keep_ref, lhs_ref, give_ref, sum_ref, total):
    i = pl.program_id(0)
    count = r_ref.shape[0]

    @pl.when(i == 0)
    def _():
        total[...] = jnp.zeros_like(total)

    r = r_ref[:, 0]
    s = r / (v_ref[0][None] - e_ref[:, 0:1][:, :, None] - 1.5 * K0)
    s_ref[:, i] = s
    keep_ref[:, i] = d_ref[:, 0]
    short = s.astype(BF16)
    lhs_ref[:count, 0] = short
    lhs_ref[count:, 0] = r.astype(BF16)
    total[...] += jnp.sum(r * s, axis=1)

    @pl.when((i == planes // 2 - 1) | (i == planes // 2))
    def _():
        give_ref[:count, 0] = short
        give_ref[count : 2 * count, 0] = r.astype(BF16)
        give_ref[2 * count :] = o_ref[...]

    @pl.when(i == planes - 1)
    def _():
        sum_ref[:count] = jnp.zeros((count, 128), F32)
        sum_ref[count:] = in_lane(jnp.sum(total[...], axis=1, keepdims=True), LANE_RS)


def prepare(residual, direction, potential, energy, mid):
    shape = residual.shape
    count, planes, rows, depth = shape
    cut = lambda fields, size: (fields, size) + tuple(shape[2:])
    middle = lambda i: jnp.clip(i - 3, 0, 1)
    outs = [cut(2 * count, planes), cut(2 * count + mid.shape[0], 2)]
    maps = [same_plane, middle]
    return pl.pallas_call(
        functools.partial(prepare_kernel, planes),
        grid=(planes,),
        in_specs=[
            plane_spec(shape, same_plane),
            plane_spec(shape, same_plane),
            pl.BlockSpec((1, rows, depth), lambda i: (i, 0, 0)),
            whole_spec(energy.shape),
            plane_spec(mid.shape, middle),
        ],
        out_specs=[DIRECT] * 2 + [plane_spec(o, m) for o, m in zip(outs, maps)] + [whole_spec((2 * count, 128))],
        out_shape=[near(shape, F32)] * 2 + [near(o, BF16) for o in outs] + [jax.ShapeDtypeStruct((2 * count, 128), F32)],
        scratch_shapes=[pltpu.VMEM((count, depth), F32)],
        compiler_params=params(8),
        cost_estimate=CHEAP,
        name="prepare",
    )(far(residual), far(direction), far(potential), energy, mid)


def corr_kernel(slots, offsets, steps, lefts, arity, sums_in, capped, masked, *refs):
    prevs, refs = refs[:sums_in], refs[sums_in:]
    if masked:
        mask_ref, refs = refs[0], refs[1:]
    lhs, refs = refs[:lefts], refs[lefts:]
    terms, out_ref, acc, top = refs[:arity], refs[arity], refs[arity + 1], refs[arity + 2]
    i = pl.program_id(0)

    @pl.when(i == 0)
    def _():
        acc[...] = jnp.zeros_like(acc)
        top[...] = jnp.zeros_like(top)

    bands = terms[0].shape[0]
    rows, depth = terms[0].shape[2], terms[0].shape[3]
    for y in range(0, rows, TILE):
        at = lambda r: r[:, 0, y : y + TILE, :].reshape(r.shape[0] * TILE, depth)
        right = jnp.concatenate([at(t) for t in terms], axis=0)
        if capped:
            size = jnp.max(jnp.abs(right.astype(F32)), axis=0, keepdims=True)
            top[...] = jnp.maximum(top[...], jnp.broadcast_to(size, top.shape))
        row = 0
        for ref in lhs:
            size = ref.shape[0] * TILE
            acc[row : row + size, :] += lax.dot_general(at(ref), right, NT, preferred_element_type=F32)
            row += size

    @pl.when(i == steps - 1)
    def _():
        width = acc.shape[1]
        row = lax.broadcasted_iota(jnp.int32, acc.shape, 0)
        col = lax.broadcasted_iota(jnp.int32, acc.shape, 1)
        same = jnp.where((row & (TILE - 1)) == (col & (TILE - 1)), acc[...], 0.0)
        red = jnp.sum(same.reshape(acc.shape[0] // TILE, TILE, width), axis=1)
        src = lax.broadcasted_iota(jnp.int32, (width, 128), 0)
        dst = lax.broadcasted_iota(jnp.int32, (width, 128), 1)
        band = src // TILE
        goal = jnp.full_like(band, -1000)
        for number, slot in enumerate(slots):
            goal = jnp.where(band // bands == number, slot * bands + band % bands, goal)
        total = prevs[0][...]
        for prev in prevs[1:]:
            total = total + prev[...]
        out_ref[...] = total
        per = red.shape[0] // len(offsets)
        for number, (top_row, lane) in enumerate(offsets):
            place = jnp.where(goal + lane == dst, 1.0, 0.0).astype(F32)
            out_ref[top_row : top_row + per, :] += exact_dot(red[number * per : (number + 1) * per], place)
        if capped:
            most = jnp.max(top[...], axis=1, keepdims=True)
            out_ref[per : 2 * per, :] += in_lane(most, LANE_CAP)
        if masked:
            out_ref[:per, :] = out_ref[:per, :] * mask_ref[...]


def correlate(prevs, lhs, offsets, terms, slots, place, steps, capped=False, mask=None):
    lhs, terms = [as_piece(a) for a in lhs], [as_piece(t) for t in terms]
    spec = lambda a: piece_spec(a, 8, place)
    fields, bands = sum(a[1][0] for a in lhs), terms[0][1][0]
    small = list(prevs) + ([] if mask is None else [mask])
    return pl.pallas_call(
        functools.partial(
            corr_kernel, slots, offsets, steps, len(lhs), len(terms), len(prevs), capped, mask is not None
        ),
        grid=(steps,),
        in_specs=[whole_spec(p.shape) for p in small] + [spec(a) for a in [*lhs, *terms]],
        out_specs=whole_spec(prevs[0].shape),
        out_shape=jax.ShapeDtypeStruct(prevs[0].shape, F32),
        scratch_shapes=[
            pltpu.VMEM((fields * TILE, len(terms) * bands * TILE), F32),
            pltpu.VMEM((8, terms[0][1][3]), F32),
        ],
        compiler_params=params(10),
        cost_estimate=CHEAP,
        name="correlate",
    )(*small, *[a[0] for a in lhs], *[t[0] for t in terms])


def band_matrix(size, period):
    row = lax.broadcasted_iota(jnp.int32, (size, size), 0)
    col = lax.broadcasted_iota(jnp.int32, (size, size), 1)
    away = jnp.abs(row - col)
    value = jnp.where(away == 1, SIDE[0], jnp.where(away == 2, SIDE[1], jnp.where(away == 3, SIDE[2], 0.0)))
    return jnp.where(row // period == col // period, value, 0.0).astype(BF16)


def coefficients(tot_ref, count):
    lane = lax.broadcasted_iota(jnp.int32, (count, 128), 1)
    return jnp.where(lane < LANE_R, tot_ref[:count], 0.0)


def scalars(tot_ref, info_ref):
    count = info_ref.shape[0]
    raw = tot_ref[:count, LANE_S : LANE_S + 32]
    product = tot_ref[count : 2 * count, LANE_RS : LANE_RS + 1]
    product = product - jnp.sum(raw * tot_ref[:count, LANE_R : LANE_R + 32], axis=1, keepdims=True)
    return product, product / info_ref[:, 0:1]


def widened(chosen, w_ref):
    count, width = chosen.shape[0], w_ref.shape[1]
    src = lax.broadcasted_iota(jnp.int32, (128, width), 0)
    dst = lax.broadcasted_iota(jnp.int32, (128, width), 1)
    spread = jnp.where(src == dst // TILE, 1.0, 0.0).astype(BF16)
    row = lax.broadcasted_iota(jnp.int32, (count, TILE, width), 1)
    col = lax.broadcasted_iota(jnp.int32, (count, TILE, width), 2)
    for half, part in enumerate(split(chosen)):
        wide = jnp.broadcast_to(dot(part, spread)[:, None, :], (count, TILE, width))
        kron = jnp.where(row == (col & (TILE - 1)), wide, 0.0)
        w_ref[half * count * TILE : (half + 1) * count * TILE, :] = kron.reshape(
            count * TILE, width
        ).astype(BF16)


def combined(w_ref, groups, plane, y):
    every = []
    for group in groups:
        parts = [
            ref[size * part : size * (part + 1), plane + first, y : y + TILE, :] for ref, size, part, first in group
        ]
        whole = parts[0]
        for part in parts[1:]:
            whole = whole + part
        every.append(whole.reshape(whole.shape[0] * TILE, whole.shape[2]))
    both = dot(w_ref[...], jnp.concatenate(every, axis=0))
    half = both.shape[0] // 2
    return (both[:half] + both[half:]).reshape(half // TILE, TILE, both.shape[1])


def grouped(refs, layout):
    groups, at = [], 0
    for group in layout:
        groups.append([(refs[at + number], *where) for number, where in enumerate(group)])
        at += len(group)
    return groups, refs[at:]


def laid_out(slots):
    flat = [as_piece(o) for group in slots for o in group]
    layout, at = [], 0
    for group in slots:
        layout.append([(o[1][0], o[2], o[3]) for o in flat[at : at + len(group)]])
        at += len(group)
    return [held(o[0]) for o in flat], layout


def direction_kernel(layout, edges, base, aliased, tot_ref, info_ref, s_ref, d_ref, *rest):
    groups, rest = grouped(rest, layout)
    if not edges:
        (lost_ref, cap_ref), rest = rest[:2], rest[2:]
    n_ref, rest = rest[aliased], rest[aliased + 1 :]
    if edges:
        side_ref, rr_ref, rest = rest[0], rest[1], rest[2:]
    w_ref, scale_ref = rest
    i = pl.program_id(0)
    count = info_ref.shape[0]

    @pl.when(i == 0)
    def _():
        product, beta = scalars(tot_ref, info_ref)
        chosen = coefficients(tot_ref, count)
        scale_ref[0] = jnp.broadcast_to(beta, scale_ref.shape[1:])
        if edges:
            rr_ref[...] = jnp.broadcast_to(product, rr_ref.shape)
        else:
            scale_ref[1] = jnp.broadcast_to(reach(chosen, cap_ref), scale_ref.shape[1:])
            chosen = chosen * info_ref[:, 2:3]
        widened(chosen, w_ref)

    beta = scale_ref[0][:, 0:1][:, :, None]
    for y in range(0, s_ref.shape[2], TILE):
        part = slice(y, y + TILE)
        new = s_ref[:, base - 3 + i, part, :] - combined(w_ref, groups, i, y)
        new = new + beta * d_ref[:, base - 3 + i, part, :]
        if edges:
            side_ref[:, 0, part, :] = new.astype(BF16)
        else:
            new = new - scale_ref[1][:, 0:1][:, :, None] * lost_ref[:, 0, part, :]
        n_ref[:, base + i, part, :] = new


def directions(tot, info, start, direction, slots, steps, base, so_far=None, lost=None, cap=None):
    shape = start.shape
    edges = lost is None
    wide = (shape[0], shape[1] + 6) + tuple(shape[2:])
    part = (shape[0], steps) + tuple(shape[2:])
    flat, layout = laid_out(slots)
    args = [tot, info, held(start), held(direction), *flat]
    in_specs = [whole_spec(tot.shape), whole_spec(info.shape)] + [DIRECT] * (2 + len(flat))
    if not edges:
        args += [lost, cap]
        in_specs += [plane_spec(part, same_plane), whole_spec(cap.shape)]
    aliases = {}
    if so_far is not None:
        aliases = {len(args): 0}
        args.append(held(so_far))
        in_specs.append(DIRECT)
    out_specs = [DIRECT]
    out_shape = [near(wide, F32)]
    if edges:
        out_specs += [plane_spec(part, same_plane), whole_spec(info.shape)]
        out_shape += [near(part, BF16), jax.ShapeDtypeStruct(info.shape, F32)]
    work = 3 if edges else 64
    return pl.pallas_call(
        functools.partial(direction_kernel, layout, edges, base, len(aliases)),
        grid=(steps,),
        in_specs=in_specs,
        out_specs=out_specs,
        out_shape=out_shape,
        input_output_aliases=aliases,
        scratch_shapes=[
            pltpu.VMEM((2 * shape[0] * TILE, len(slots) * layout[0][0][0] * TILE), BF16),
            pltpu.VMEM((2, shape[0], 128), F32),
        ],
        compiler_params=params(6),
        cost_estimate=pl.CostEstimate(
            flops=steps * 2 * 256 * 1024 * 384, bytes_accessed=work * MIB, transcendentals=0
        ),
        name="directions",
    )(*args)


def reach(chosen, cap_ref):
    count = chosen.shape[0]
    cap = cap_ref[count : 2 * count, LANE_CAP : LANE_CAP + 1]
    return jnp.maximum(jnp.sum(jnp.abs(chosen), axis=1, keepdims=True) * cap, 1e-30)


def removal_kernel(layout, tot_ref, cap_ref, *rest):
    groups, (out_ref, w_ref) = grouped(rest, layout)

    @pl.when(pl.program_id(0) == 0)
    def _():
        chosen = coefficients(tot_ref, out_ref.shape[0])
        widened(chosen / reach(chosen, cap_ref), w_ref)

    for y in range(0, out_ref.shape[2], TILE):
        out_ref[:, 0, y : y + TILE, :] = combined(w_ref, groups, pl.program_id(0), y)


def removals(tot, cap, slots, count):
    flat, layout = laid_out(slots)
    shape = (count,) + tuple(as_piece(slots[0][0])[1][1:])
    return pl.pallas_call(
        functools.partial(removal_kernel, layout),
        grid=(shape[1],),
        in_specs=[whole_spec(tot.shape), whole_spec(cap.shape)] + [DIRECT] * len(flat),
        out_specs=plane_spec(shape, same_plane),
        out_shape=near(shape, F32),
        scratch_shapes=[
            pltpu.VMEM((2 * count * TILE, len(slots) * layout[0][0][0] * TILE), BF16),
        ],
        compiler_params=params(6),
        cost_estimate=pl.CostEstimate(
            flops=2 * 2 * 256 * 1024 * 384, bytes_accessed=4 * MIB, transcendentals=0
        ),
        name="removals",
    )(tot, cap, *flat)


def image_kernel(
    planes, info_ref, low_ref, high_ref, v_ref, wide_in, r_ref, x_ref,
    new_ref, image_ref, curve_ref, keep_ref, n_ref, r_near, x_near, ky, even, odd, total, sem,
):
    i = pl.program_id(0)
    count, _, rows, depth = n_ref.shape

    @pl.when(i == 0)
    def _():
        ky[...] = band_matrix(count * rows, rows)
        total[...] = jnp.zeros_like(total)
        pltpu.make_async_copy(r_ref, r_near, sem.at[0]).start()
        pltpu.make_async_copy(x_ref, x_near, sem.at[1]).start()
        n_ref[:, 0:3] = low_ref[...].astype(F32)
        n_ref[:, planes + 3 : planes + 6] = high_ref[...].astype(F32)

    lane = lax.broadcasted_iota(jnp.int32, (rows, depth), 1)
    for half, beside in enumerate((even, odd)):
        high, low = split(n_ref[:, 2 * i + half + 3].reshape(count * rows, depth))
        beside[...] = (dot(ky[...], high) + dot(ky[...], low)).reshape(beside.shape)
    for half, beside in enumerate((even, odd)):
        plane = 2 * i + half + 3
        shifted = v_ref[half] - 1.5 * K0
        for c in range(count):
            here = n_ref[c, plane]
            side = beside[c]
            for away in range(1, 4):
                below = jnp.where(lane >= away, pltpu.roll(here, away, 1), 0.0)
                above = jnp.where(lane < depth - away, pltpu.roll(here, depth - away, 1), 0.0)
                pair = n_ref[c, plane - away] + n_ref[c, plane + away]
                side = side + SIDE[away - 1] * (below + above + pair)
            image = SCALE * side + (shifted - info_ref[c : c + 1, 1:2]) * here
            new_ref[c, half] = here
            keep_ref[c, plane - 3] = here
            image_ref[c, plane - 3] = image
            total[c : c + 1] += jnp.sum(here * image, axis=0, keepdims=True)

    @pl.when(i == planes // 2 - 1)
    def _():
        curve_ref[...] = jnp.broadcast_to(jnp.sum(total[...], axis=1, keepdims=True), curve_ref.shape)
        pltpu.make_async_copy(r_ref, r_near, sem.at[0]).wait()
        pltpu.make_async_copy(x_ref, x_near, sem.at[1]).wait()


def images(info, low, wide, high, potential, residual, solution):
    count, _, rows, depth = wide.shape
    planes = potential.shape[0]
    shape = (count, planes, rows, depth)
    return pl.pallas_call(
        functools.partial(image_kernel, planes),
        grid=(planes // 2,),
        in_specs=[
            whole_spec(info.shape), DIRECT, DIRECT,
            pl.BlockSpec((2, rows, depth), lambda i: (i, 0, 0)),
            DIRECT,
        ]
        + [pl.BlockSpec(memory_space=pl.ANY)] * 2,
        out_specs=[
            pl.BlockSpec((count, 2, rows, depth), lambda i: (0, i, 0, 0)), DIRECT, whole_spec((count, 128)),
        ]
        + [DIRECT] * 4,
        out_shape=[
            pltpu.HBM(shape, F32), near(shape, F32), jax.ShapeDtypeStruct((count, 128), F32),
            near(shape, F32), near(wide.shape, F32), near(shape, F32), near(shape, F32),
        ],
        input_output_aliases={4: 4},
        scratch_shapes=[
            pltpu.VMEM((count * rows, count * rows), BF16),
            pltpu.VMEM((count, rows, depth), F32),
            pltpu.VMEM((count, rows, depth), F32),
            pltpu.VMEM((count, depth), F32),
            pltpu.SemaphoreType.DMA((2,)),
        ],
        compiler_params=params(8),
        cost_estimate=pl.CostEstimate(flops=4 * 10**9, bytes_accessed=24 * MIB, transcendentals=0),
        name="images",
    )(info, held(low), held(high), far(potential), held(wide), far(residual), far(solution))


def finish_kernel(planes, tot_ref, info_ref, curve_ref, n_ref, image_ref, r_ref, x_ref, sol_ref, res_ref, sol, res, sem):
    product, _ = scalars(tot_ref, info_ref)
    size = jnp.broadcast_to(product / curve_ref[:, 0:1], info_ref.shape)[:, 0:1][:, :, None]
    copies = []
    for plane in range(planes):
        sol[:, plane] = x_ref[:, plane] + size * n_ref[:, plane]
        res[:, plane] = r_ref[:, plane] - size * image_ref[:, plane]
        for number, (source, target) in enumerate(((sol, sol_ref), (res, res_ref))):
            copy = pltpu.make_async_copy(source.at[:, plane], target.at[:, plane], sem.at[number, plane])
            copy.start()
            copies.append(copy)
    for copy in copies:
        copy.wait()


def finish(tot, info, curve, new, image, residual, solution):
    shape = new.shape
    return pl.pallas_call(
        functools.partial(finish_kernel, shape[1]),
        in_specs=[DIRECT] * 7,
        out_specs=[pl.BlockSpec(memory_space=pl.ANY)] * 2,
        out_shape=[pltpu.HBM(shape, F32)] * 2,
        scratch_shapes=[pltpu.VMEM(shape, F32)] * 2 + [pltpu.SemaphoreType.DMA((2, shape[1]))],
        compiler_params=params(8),
        name="finish",
    )(tot, info, curve, held(new), held(image), held(residual), held(solution))


def after(value, *others):
    return lax.optimization_barrier((value, *others))[0]


SWAP = [(0, 1), (1, 0), (2, 3), (3, 2)]
INNER = [(1, 2), (2, 1)]
INWARD = [(0, 1), (3, 2)]
OUTWARD = [(1, 0), (2, 3)]


def grid_sum(value):
    size = lax.axis_size("grid")
    away = lambda x, step: lax.ppermute(x, "grid", [(i, i ^ step) for i in range(size)])
    value = value + away(value, 1)
    stride = 2
    while stride < size:
        if 4 * stride <= size:
            near_by, above, across = (away(value, step * stride) for step in (1, 2, 3))
            value = (value + near_by) + (above + across)
            stride *= 4
        else:
            value = value + away(value, stride)
            stride *= 2
    return value


def hop(value, pairs):
    return lax.ppermute(value, "band", pairs)


def on_device(
    residual,
    direction,
    solution,
    old_product,
    orbitals,
    energies,
    potential,
    column_index,
    panel_index,
):
    count = residual.shape[0]
    bands = orbitals.shape[0]
    groups = lax.axis_size("band")
    place = lax.axis_index("band")
    is_end = (place == 0) | (place == groups - 1)
    ends = lax.axis_size("grid") - 1
    upward = [(i, i + 1) for i in range(ends)]
    downward = [(i + 1, i) for i in range(ends)]
    used = groups * bands

    halves = (orbitals[:, 0:3], orbitals[:, 5:8])
    mid = orbitals[:, 3:5]
    edge_pair = [hop(half, SWAP) for half in halves]
    edge_inner = hop(jnp.concatenate(halves, axis=1), INNER)
    sides = lambda x: [piece(x, bands, 0, 0), piece(x, bands, 0, 3)]

    band_ids = lax.iota(jnp.int32, energies.shape[0])
    picked = jnp.where(
        band_ids[None, :] == (column_index // 3)[:, None], energies[None, :], jnp.float32(0.0)
    )
    energy = jnp.sum(picked, axis=1)
    wide_energy = jnp.broadcast_to(energy[:, None], (count, 128))
    start, direction, lhs, give, tot = prepare(residual, direction, potential, wide_energy, mid)
    lhs = held(lhs)
    kinds = ((0, LANE_S), (0, LANE_R))
    places = (same_plane, high_plane)
    tot = correlate([tot], [lhs], kinds, [far(orbitals)], (0,), edge_plane, 6)

    edge_far = [hop(after(half, tot), INNER) for half in edge_pair]
    edge_next = hop(after(edge_inner, tot), OUTWARD)
    got = hop(give, INWARD)
    for pair, inner, where in zip(edge_pair, sides(edge_inner), places):
        tot = correlate([tot], [lhs], kinds, [pair, inner], (1, 2), where, 3)

    edge_last = [hop(after(edge_far[0], tot), OUTWARD), hop(after(edge_far[1], tot, edge_next), OUTWARD)]
    both = hop(jnp.concatenate([mid, after(got, tot, *edge_far)[2 * count :]]), INNER)
    mid_pair, mid_inner, mid_far = piece(got, bands, 2 * count // bands), piece(both, bands, 0), piece(both, bands, 1)
    mids = [mid, mid_pair, mid_inner, mid_far]
    for nearer, farther, where in zip(sides(edge_next), edge_far, places):
        tot = correlate([tot], [lhs], kinds, [nearer, farther], (2, 3), where, 3)
    given = correlate(
        [jnp.zeros((2 * count, 128), F32)], [piece(got, 2 * count, 0)], kinds,
        [mid, mid_inner, mid_far, mid_pair], (1, 2, 3, -100), same_plane, 2, True,
    )
    tot = correlate([tot], [lhs], kinds, mids, (0, 1, 2, 3), mid_plane, 2)
    taken = hop(after(given, tot), OUTWARD)
    tot = correlate([tot], [lhs], kinds, [edge_last[0]], (3,), same_plane, 3)

    lane = lax.iota(jnp.int32, 128)
    group = jnp.where(
        place < groups // 2,
        jnp.stack([place, 1 - place, jnp.int32(2), jnp.int32(3)]),
        jnp.stack([place, 5 - place, jnp.int32(1), jnp.int32(0)]),
    )
    ids = (group[:, None] * bands + lax.iota(jnp.int32, bands)[None, :]).reshape(used)
    cells = float(residual.shape[1] * lax.axis_size("grid") * residual.shape[2] * residual.shape[3])
    member = jnp.where(ids[None, :] // PB == panel_index[:, None], jnp.float32(1.0 / cells), jnp.float32(0.0))
    member = jnp.pad(member, ((0, 0), (0, 128 - used)), constant_values=1.0)
    inside = jnp.where(is_end, 0.0, 1.0)
    info = jnp.where(
        lane[None, :] == 0,
        old_product[:, None],
        jnp.where(lane[None, :] == 1, energy[:, None], inside),
    )
    cap = given * inside + taken
    tot, cap, info, member = lax.optimization_barrier((tot, cap, info, member))
    tot = correlate([tot, taken], [lhs], kinds, [edge_last[1]], (3,), high_plane, 3, False, member)
    tot = grid_sum(tot)

    slots = [
        [[halves[half]], [edge_pair[half]], [inner, nearer], [edge_far[half], edge_last[half]]]
        for half, inner, nearer in zip(range(2), sides(edge_inner), sides(edge_next))
    ]
    other_tot = hop(tot, INWARD)
    wide, low, product = directions(tot, info, start, direction, slots[0], 3, 3)
    from_right = lax.ppermute(low, "grid", downward)
    lost = removals(after(other_tot, low), cap, [[mid_pair], [mid], [mid_inner], [mid_far]], count)
    lost = (lost * jnp.float32(TOP)).astype(jnp.float16)
    wide, high, _ = directions(after(tot, lost), info, start, direction, slots[1], 3, 8, wide)
    from_left = lax.ppermute(high, "grid", upward)
    lost = hop(lost, OUTWARD).astype(F32) * jnp.float32(1.0 / TOP)
    (wide,) = directions(
        tot, info, start, direction, [[m] for m in mids], 2, 6, wide, lost, cap
    )
    new, image, curve, keep, _, residual, solution = images(
        info, from_left, wide, from_right, potential, residual, solution
    )
    curve = grid_sum(curve)
    new_solution, new_residual = finish(tot, info, curve, keep, image, residual, solution)
    return new_solution, new_residual, new, product[:, 0]


def solution(mesh):
    tiles = P("band", "grid", None, None)
    return jax.shard_map(
        on_device,
        mesh=mesh,
        in_specs=(tiles, tiles, tiles, P("band"), tiles, P(), P("grid", None, None), P("band"), P("band")),
        out_specs=(tiles, tiles, tiles, P("band")),
        check_vma=False,
    )
```

```python
import functools

import jax
import jax.numpy as jnp
from jax import lax
from jax.experimental import pallas as pl
from jax.experimental.pallas import tpu as pltpu
from jax.sharding import PartitionSpec as P

PB = 16
K0 = -49.0 / 18.0
SIDE = (270.0, -27.0, 2.0)
SCALE = -0.5 / 180.0
F32, BF16 = jnp.float32, jnp.bfloat16
TILE = 16
MIB = 1 << 20
TOP = 16384.0
NT = (((1,), (1,)), ((), ()))
LANE_S, LANE_R, LANE_RS, LANE_CAP = 0, 32, 96, 100


def edge_plane(i):
    return i + 2 * (i // 3)


def high_plane(i):
    return i + 5


def mid_plane(i):
    return i + 3


def same_plane(i):
    return i


def plane_spec(shape, place, part=0):
    return pl.BlockSpec((shape[0], 1) + tuple(shape[2:]), lambda i: (part, place(i), 0, 0))


def piece(array, size, part, first=0):
    return array, (size,) + tuple(array.shape[1:]), part, first


def as_piece(x):
    return x if isinstance(x, tuple) else piece(x, x.shape[0], 0)


def piece_spec(x, planes, place):
    array, shape, part, first = x
    return plane_spec(shape, place if shape[1] == planes else (lambda i: i + first), part)


def whole_spec(shape):
    return pl.BlockSpec(tuple(shape), lambda i: (0,) * len(shape))


def params(limit):
    return pltpu.CompilerParams(vmem_limit_bytes=limit * MIB)


CHEAP = pl.CostEstimate(flops=10**6, bytes_accessed=MIB, transcendentals=0)


DIRECT = pl.BlockSpec(memory_space=pltpu.VMEM)


def near(shape, dtype):
    return pltpu.VMEM(tuple(shape), dtype)


def far(x):
    return pltpu.with_memory_space_constraint(x, pltpu.HBM)


def held(x):
    return pltpu.with_memory_space_constraint(x, pltpu.VMEM)


def dot(a, b):
    return jnp.dot(a, b, preferred_element_type=F32)


def exact_dot(a, b):
    return jnp.dot(a, b, precision=lax.Precision.HIGHEST, preferred_element_type=F32)


def split(x):
    high = x.astype(BF16)
    return high, (x - high.astype(F32)).astype(BF16)


def in_lane(column, lane):
    at = lax.broadcasted_iota(jnp.int32, (column.shape[0], 128), 1)
    return jnp.where(at == lane, column, 0.0)


def prepare_kernel(planes, r_ref, d_ref, v_ref, e_ref, o_ref, s_ref, keep_ref, lhs_ref, give_ref, sum_ref, total):
    i = pl.program_id(0)
    count = r_ref.shape[0]

    @pl.when(i == 0)
    def _():
        total[...] = jnp.zeros_like(total)

    r = r_ref[:, 0]
    s = r / (v_ref[0][None] - e_ref[:, 0:1][:, :, None] - 1.5 * K0)
    s_ref[:, i] = s
    keep_ref[:, i] = d_ref[:, 0]
    short = s.astype(BF16)
    lhs_ref[:count, 0] = short
    lhs_ref[count:, 0] = r.astype(BF16)
    total[...] += jnp.sum(r * s, axis=1)

    @pl.when((i == planes // 2 - 1) | (i == planes // 2))
    def _():
        give_ref[:count, 0] = short
        give_ref[count : 2 * count, 0] = r.astype(BF16)
        give_ref[2 * count :] = o_ref[...]

    @pl.when(i == planes - 1)
    def _():
        sum_ref[:count] = jnp.zeros((count, 128), F32)
        sum_ref[count:] = in_lane(jnp.sum(total[...], axis=1, keepdims=True), LANE_RS)


def prepare(residual, direction, potential, energy, mid):
    shape = residual.shape
    count, planes, rows, depth = shape
    cut = lambda fields, size: (fields, size) + tuple(shape[2:])
    middle = lambda i: jnp.clip(i - 3, 0, 1)
    outs = [cut(2 * count, planes), cut(2 * count + mid.shape[0], 2)]
    maps = [same_plane, middle]
    return pl.pallas_call(
        functools.partial(prepare_kernel, planes),
        grid=(planes,),
        in_specs=[
            plane_spec(shape, same_plane),
            plane_spec(shape, same_plane),
            pl.BlockSpec((1, rows, depth), lambda i: (i, 0, 0)),
            whole_spec(energy.shape),
            plane_spec(mid.shape, middle),
        ],
        out_specs=[DIRECT] * 2 + [plane_spec(o, m) for o, m in zip(outs, maps)] + [whole_spec((2 * count, 128))],
        out_shape=[near(shape, F32)] * 2 + [near(o, BF16) for o in outs] + [jax.ShapeDtypeStruct((2 * count, 128), F32)],
        scratch_shapes=[pltpu.VMEM((count, depth), F32)],
        compiler_params=params(8),
        cost_estimate=CHEAP,
        name="prepare",
    )(far(residual), far(direction), far(potential), energy, mid)


def corr_kernel(slots, offsets, steps, lefts, arity, sums_in, capped, masked, *refs):
    prevs, refs = refs[:sums_in], refs[sums_in:]
    if masked:
        mask_ref, refs = refs[0], refs[1:]
    lhs, refs = refs[:lefts], refs[lefts:]
    terms, out_ref, acc, top = refs[:arity], refs[arity], refs[arity + 1], refs[arity + 2]
    i = pl.program_id(0)

    @pl.when(i == 0)
    def _():
        acc[...] = jnp.zeros_like(acc)
        top[...] = jnp.zeros_like(top)

    bands = terms[0].shape[0]
    rows, depth = terms[0].shape[2], terms[0].shape[3]
    for y in range(0, rows, TILE):
        at = lambda r: r[:, 0, y : y + TILE, :].reshape(r.shape[0] * TILE, depth)
        right = jnp.concatenate([at(t) for t in terms], axis=0)
        if capped:
            size = jnp.max(jnp.abs(right.astype(F32)), axis=0, keepdims=True)
            top[...] = jnp.maximum(top[...], jnp.broadcast_to(size, top.shape))
        row = 0
        for ref in lhs:
            size = ref.shape[0] * TILE
            acc[row : row + size, :] += lax.dot_general(at(ref), right, NT, preferred_element_type=F32)
            row += size

    @pl.when(i == steps - 1)
    def _():
        width = acc.shape[1]
        row = lax.broadcasted_iota(jnp.int32, acc.shape, 0)
        col = lax.broadcasted_iota(jnp.int32, acc.shape, 1)
        same = jnp.where((row & (TILE - 1)) == (col & (TILE - 1)), acc[...], 0.0)
        red = jnp.sum(same.reshape(acc.shape[0] // TILE, TILE, width), axis=1)
        src = lax.broadcasted_iota(jnp.int32, (width, 128), 0)
        dst = lax.broadcasted_iota(jnp.int32, (width, 128), 1)
        band = src // TILE
        goal = jnp.full_like(band, -1000)
        for number, slot in enumerate(slots):
            goal = jnp.where(band // bands == number, slot * bands + band % bands, goal)
        total = prevs[0][...]
        for prev in prevs[1:]:
            total = total + prev[...]
        out_ref[...] = total
        per = red.shape[0] // len(offsets)
        for number, (top_row, lane) in enumerate(offsets):
            place = jnp.where(goal + lane == dst, 1.0, 0.0).astype(F32)
            out_ref[top_row : top_row + per, :] += exact_dot(red[number * per : (number + 1) * per], place)
        if capped:
            most = jnp.max(top[...], axis=1, keepdims=True)
            out_ref[per : 2 * per, :] += in_lane(most, LANE_CAP)
        if masked:
            out_ref[:per, :] = out_ref[:per, :] * mask_ref[...]


def correlate(prevs, lhs, offsets, terms, slots, place, steps, capped=False, mask=None):
    lhs, terms = [as_piece(a) for a in lhs], [as_piece(t) for t in terms]
    spec = lambda a: piece_spec(a, 8, place)
    fields, bands = sum(a[1][0] for a in lhs), terms[0][1][0]
    small = list(prevs) + ([] if mask is None else [mask])
    return pl.pallas_call(
        functools.partial(
            corr_kernel, slots, offsets, steps, len(lhs), len(terms), len(prevs), capped, mask is not None
        ),
        grid=(steps,),
        in_specs=[whole_spec(p.shape) for p in small] + [spec(a) for a in [*lhs, *terms]],
        out_specs=whole_spec(prevs[0].shape),
        out_shape=jax.ShapeDtypeStruct(prevs[0].shape, F32),
        scratch_shapes=[
            pltpu.VMEM((fields * TILE, len(terms) * bands * TILE), F32),
            pltpu.VMEM((8, terms[0][1][3]), F32),
        ],
        compiler_params=params(10),
        cost_estimate=CHEAP,
        name="correlate",
    )(*small, *[a[0] for a in lhs], *[t[0] for t in terms])


def band_matrix(size, period):
    row = lax.broadcasted_iota(jnp.int32, (size, size), 0)
    col = lax.broadcasted_iota(jnp.int32, (size, size), 1)
    away = jnp.abs(row - col)
    value = jnp.where(away == 1, SIDE[0], jnp.where(away == 2, SIDE[1], jnp.where(away == 3, SIDE[2], 0.0)))
    return jnp.where(row // period == col // period, value, 0.0).astype(BF16)


def coefficients(tot_ref, count):
    lane = lax.broadcasted_iota(jnp.int32, (count, 128), 1)
    return jnp.where(lane < LANE_R, tot_ref[:count], 0.0)


def scalars(tot_ref, info_ref):
    count = info_ref.shape[0]
    raw = tot_ref[:count, LANE_S : LANE_S + 32]
    product = tot_ref[count : 2 * count, LANE_RS : LANE_RS + 1]
    product = product - jnp.sum(raw * tot_ref[:count, LANE_R : LANE_R + 32], axis=1, keepdims=True)
    return product, product / info_ref[:, 0:1]


def widened(chosen, w_ref):
    count, width = chosen.shape[0], w_ref.shape[1]
    src = lax.broadcasted_iota(jnp.int32, (128, width), 0)
    dst = lax.broadcasted_iota(jnp.int32, (128, width), 1)
    spread = jnp.where(src == dst // TILE, 1.0, 0.0).astype(BF16)
    row = lax.broadcasted_iota(jnp.int32, (count, TILE, width), 1)
    col = lax.broadcasted_iota(jnp.int32, (count, TILE, width), 2)
    for half, part in enumerate(split(chosen)):
        wide = jnp.broadcast_to(dot(part, spread)[:, None, :], (count, TILE, width))
        kron = jnp.where(row == (col & (TILE - 1)), wide, 0.0)
        w_ref[half * count * TILE : (half + 1) * count * TILE, :] = kron.reshape(
            count * TILE, width
        ).astype(BF16)


def combined(w_ref, groups, plane, y):
    every = []
    for group in groups:
        parts = [
            ref[size * part : size * (part + 1), plane + first, y : y + TILE, :] for ref, size, part, first in group
        ]
        whole = parts[0]
        for part in parts[1:]:
            whole = whole + part
        every.append(whole.reshape(whole.shape[0] * TILE, whole.shape[2]))
    both = dot(w_ref[...], jnp.concatenate(every, axis=0))
    half = both.shape[0] // 2
    return (both[:half] + both[half:]).reshape(half // TILE, TILE, both.shape[1])


def grouped(refs, layout):
    groups, at = [], 0
    for group in layout:
        groups.append([(refs[at + number], *where) for number, where in enumerate(group)])
        at += len(group)
    return groups, refs[at:]


def laid_out(slots):
    flat = [as_piece(o) for group in slots for o in group]
    layout, at = [], 0
    for group in slots:
        layout.append([(o[1][0], o[2], o[3]) for o in flat[at : at + len(group)]])
        at += len(group)
    return [held(o[0]) for o in flat], layout


def direction_kernel(layout, first, edges, base, aliased, *refs):
    if first:
        (tot_ref, info_ref, cap_ref), refs = refs[:3], refs[3:]
    else:
        (info_ref, w_ref, scale_ref), refs = refs[:3], refs[3:]
    (s_ref, d_ref), rest = refs[:2], refs[2:]
    groups, rest = grouped(rest, layout)
    if not edges:
        lost_ref, rest = rest[0], rest[1:]
    n_ref, rest = rest[aliased], rest[aliased + 1 :]
    if edges:
        side_ref, rest = rest[0], rest[1:]
    i = pl.program_id(0)
    count = info_ref.shape[0]

    if first:
        w_ref, scale_ref = rest

        @pl.when(i == 0)
        def _():
            product, beta = scalars(tot_ref, info_ref)
            chosen = coefficients(tot_ref, count)
            for number, column in enumerate((beta, reach(chosen, cap_ref), product)):
                scale_ref[number] = jnp.broadcast_to(column, scale_ref.shape[1:])
            widened(chosen, w_ref)

    beta = scale_ref[0][:, 0:1][:, :, None]
    for y in range(0, s_ref.shape[2], TILE):
        part = slice(y, y + TILE)
        removed = combined(w_ref, groups, i, y)
        if not edges:
            removed = info_ref[:, 2:3][:, :, None] * removed
            removed = removed + scale_ref[1][:, 0:1][:, :, None] * lost_ref[:, 0, part, :]
        new = s_ref[:, base - 3 + i, part, :] - removed + beta * d_ref[:, base - 3 + i, part, :]
        if edges:
            side_ref[:, 0, part, :] = new.astype(BF16)
        n_ref[:, base + i, part, :] = new


def directions(scalings, info, start, direction, slots, steps, base, so_far=None, lost=None):
    shape = start.shape
    first, edges = so_far is None, lost is None
    wide = (shape[0], shape[1] + 6) + tuple(shape[2:])
    part = (shape[0], steps) + tuple(shape[2:])
    flat, layout = laid_out(slots)
    if first:
        tot, cap = scalings
        args = [tot, info, cap]
        in_specs = [whole_spec(a.shape) for a in args]
    else:
        args = [info, held(scalings[0]), held(scalings[1])]
        in_specs = [whole_spec(info.shape), DIRECT, DIRECT]
    args += [held(start), held(direction), *flat]
    in_specs += [DIRECT] * (2 + len(flat))
    if not edges:
        args.append(lost)
        in_specs.append(plane_spec(part, same_plane))
    aliases = {}
    if not first:
        aliases = {len(args): 0}
        args.append(held(so_far))
        in_specs.append(DIRECT)
    out_specs, out_shape = [DIRECT], [near(wide, F32)]
    if edges:
        out_specs.append(plane_spec(part, same_plane))
        out_shape.append(near(part, BF16))
    if first:
        out_specs += [DIRECT, DIRECT]
        out_shape += [
            near((2 * shape[0] * TILE, len(slots) * layout[0][0][0] * TILE), BF16),
            near((3, shape[0], 128), F32),
        ]
    work = 3 if edges else 64
    return pl.pallas_call(
        functools.partial(direction_kernel, layout, first, edges, base, len(aliases)),
        grid=(steps,),
        in_specs=in_specs,
        out_specs=out_specs,
        out_shape=out_shape,
        input_output_aliases=aliases,
        compiler_params=params(6),
        cost_estimate=pl.CostEstimate(
            flops=steps * 2 * 256 * 1024 * 384, bytes_accessed=work * MIB, transcendentals=0
        ),
        name="directions",
    )(*args)


def reach(chosen, cap_ref):
    count = chosen.shape[0]
    cap = cap_ref[count : 2 * count, LANE_CAP : LANE_CAP + 1]
    return jnp.maximum(jnp.sum(jnp.abs(chosen), axis=1, keepdims=True) * cap, 1e-30)


def removal_kernel(layout, tot_ref, cap_ref, *rest):
    groups, (out_ref, w_ref) = grouped(rest, layout)

    @pl.when(pl.program_id(0) == 0)
    def _():
        chosen = coefficients(tot_ref, out_ref.shape[0])
        widened(chosen / reach(chosen, cap_ref), w_ref)

    for y in range(0, out_ref.shape[2], TILE):
        out_ref[:, 0, y : y + TILE, :] = combined(w_ref, groups, pl.program_id(0), y)


def removals(tot, cap, slots, count):
    flat, layout = laid_out(slots)
    shape = (count,) + tuple(as_piece(slots[0][0])[1][1:])
    return pl.pallas_call(
        functools.partial(removal_kernel, layout),
        grid=(shape[1],),
        in_specs=[whole_spec(tot.shape), whole_spec(cap.shape)] + [DIRECT] * len(flat),
        out_specs=plane_spec(shape, same_plane),
        out_shape=near(shape, F32),
        scratch_shapes=[
            pltpu.VMEM((2 * count * TILE, len(slots) * layout[0][0][0] * TILE), BF16),
        ],
        compiler_params=params(6),
        cost_estimate=pl.CostEstimate(
            flops=2 * 2 * 256 * 1024 * 384, bytes_accessed=4 * MIB, transcendentals=0
        ),
        name="removals",
    )(tot, cap, *flat)


def image_kernel(
    planes, info_ref, low_ref, high_ref, v_ref, wide_in, r_ref, x_ref,
    new_ref, image_ref, curve_ref, keep_ref, n_ref, r_near, x_near, ky, kz, even, odd, total, sem,
):
    i = pl.program_id(0)
    count, _, rows, depth = n_ref.shape

    @pl.when(i == 0)
    def _():
        ky[...] = band_matrix(count * rows, rows)
        kz[...] = band_matrix(depth, depth)
        total[...] = jnp.zeros_like(total)
        pltpu.make_async_copy(r_ref, r_near, sem.at[0]).start()
        pltpu.make_async_copy(x_ref, x_near, sem.at[1]).start()
        n_ref[:, 0:3] = low_ref[...].astype(F32)
        n_ref[:, planes + 3 : planes + 6] = high_ref[...].astype(F32)

    for half, beside in enumerate((even, odd)):
        high, low = split(n_ref[:, 2 * i + half + 3].reshape(count * rows, depth))
        sides = dot(ky[...], high) + dot(ky[...], low) + dot(high, kz[...]) + dot(low, kz[...])
        beside[...] = sides.reshape(beside.shape)
    for half, beside in enumerate((even, odd)):
        plane = 2 * i + half + 3
        shifted = v_ref[half] - 1.5 * K0
        for c in range(count):
            here = n_ref[c, plane]
            side = beside[c]
            for away in range(1, 4):
                side = side + SIDE[away - 1] * (n_ref[c, plane - away] + n_ref[c, plane + away])
            image = SCALE * side + (shifted - info_ref[c : c + 1, 1:2]) * here
            new_ref[c, half] = here
            keep_ref[c, plane - 3] = here
            image_ref[c, plane - 3] = image
            total[c : c + 1] += jnp.sum(here * image, axis=0, keepdims=True)

    @pl.when(i == planes // 2 - 1)
    def _():
        curve_ref[...] = jnp.broadcast_to(jnp.sum(total[...], axis=1, keepdims=True), curve_ref.shape)
        pltpu.make_async_copy(r_ref, r_near, sem.at[0]).wait()
        pltpu.make_async_copy(x_ref, x_near, sem.at[1]).wait()


def images(info, low, wide, high, potential, residual, solution):
    count, _, rows, depth = wide.shape
    planes = potential.shape[0]
    shape = (count, planes, rows, depth)
    return pl.pallas_call(
        functools.partial(image_kernel, planes),
        grid=(planes // 2,),
        in_specs=[
            whole_spec(info.shape), DIRECT, DIRECT,
            pl.BlockSpec((2, rows, depth), lambda i: (i, 0, 0)),
            DIRECT,
        ]
        + [pl.BlockSpec(memory_space=pl.ANY)] * 2,
        out_specs=[
            pl.BlockSpec((count, 2, rows, depth), lambda i: (0, i, 0, 0)), DIRECT, whole_spec((count, 128)),
        ]
        + [DIRECT] * 4,
        out_shape=[
            pltpu.HBM(shape, F32), near(shape, F32), jax.ShapeDtypeStruct((count, 128), F32),
            near(shape, F32), near(wide.shape, F32), near(shape, F32), near(shape, F32),
        ],
        input_output_aliases={4: 4},
        scratch_shapes=[
            pltpu.VMEM((count * rows, count * rows), BF16),
            pltpu.VMEM((depth, depth), BF16),
            pltpu.VMEM((count, rows, depth), F32),
            pltpu.VMEM((count, rows, depth), F32),
            pltpu.VMEM((count, depth), F32),
            pltpu.SemaphoreType.DMA((2,)),
        ],
        compiler_params=params(8),
        cost_estimate=pl.CostEstimate(flops=4 * 10**9, bytes_accessed=24 * MIB, transcendentals=0),
        name="images",
    )(info, held(low), held(high), far(potential), held(wide), far(residual), far(solution))


def finish_kernel(planes, tot_ref, info_ref, curve_ref, n_ref, image_ref, r_ref, x_ref, sol_ref, res_ref, sol, res, sem):
    product, _ = scalars(tot_ref, info_ref)
    size = jnp.broadcast_to(product / curve_ref[:, 0:1], info_ref.shape)[:, 0:1][:, :, None]
    copies = []
    for plane in range(planes):
        sol[:, plane] = x_ref[:, plane] + size * n_ref[:, plane]
        res[:, plane] = r_ref[:, plane] - size * image_ref[:, plane]
        for number, (source, target) in enumerate(((sol, sol_ref), (res, res_ref))):
            copy = pltpu.make_async_copy(source.at[:, plane], target.at[:, plane], sem.at[number, plane])
            copy.start()
            copies.append(copy)
    for copy in copies:
        copy.wait()


def finish(tot, info, curve, new, image, residual, solution):
    shape = new.shape
    return pl.pallas_call(
        functools.partial(finish_kernel, shape[1]),
        in_specs=[DIRECT] * 7,
        out_specs=[pl.BlockSpec(memory_space=pl.ANY)] * 2,
        out_shape=[pltpu.HBM(shape, F32)] * 2,
        scratch_shapes=[pltpu.VMEM(shape, F32)] * 2 + [pltpu.SemaphoreType.DMA((2, shape[1]))],
        compiler_params=params(8),
        name="finish",
    )(tot, info, curve, held(new), held(image), held(residual), held(solution))


def after(value, *others):
    return lax.optimization_barrier((value, *others))[0]


SWAP = [(0, 1), (1, 0), (2, 3), (3, 2)]
INNER = [(1, 2), (2, 1)]
INWARD = [(0, 1), (3, 2)]
OUTWARD = [(1, 0), (2, 3)]


def grid_sum(value):
    size = lax.axis_size("grid")
    away = lambda x, step: lax.ppermute(x, "grid", [(i, i ^ step) for i in range(size)])
    value = value + away(value, 1)
    stride = 2
    while stride < size:
        if 4 * stride <= size:
            near_by, above, across = (away(value, step * stride) for step in (1, 2, 3))
            value = (value + near_by) + (above + across)
            stride *= 4
        else:
            value = value + away(value, stride)
            stride *= 2
    return value


def hop(value, pairs):
    return lax.ppermute(value, "band", pairs)


def on_device(
    residual,
    direction,
    solution,
    old_product,
    orbitals,
    energies,
    potential,
    column_index,
    panel_index,
):
    count = residual.shape[0]
    bands = orbitals.shape[0]
    groups = lax.axis_size("band")
    place = lax.axis_index("band")
    is_end = (place == 0) | (place == groups - 1)
    ends = lax.axis_size("grid") - 1
    upward = [(i, i + 1) for i in range(ends)]
    downward = [(i + 1, i) for i in range(ends)]
    used = groups * bands

    halves = (orbitals[:, 0:3], orbitals[:, 5:8])
    mid = orbitals[:, 3:5]
    edge_pair = [hop(half, SWAP) for half in halves]
    edge_inner = hop(jnp.concatenate(halves, axis=1), INNER)
    sides = lambda x: [piece(x, bands, 0, 0), piece(x, bands, 0, 3)]

    band_ids = lax.iota(jnp.int32, energies.shape[0])
    picked = jnp.where(
        band_ids[None, :] == (column_index // 3)[:, None], energies[None, :], jnp.float32(0.0)
    )
    energy = jnp.sum(picked, axis=1)
    wide_energy = jnp.broadcast_to(energy[:, None], (count, 128))
    start, direction, lhs, give, tot = prepare(residual, direction, potential, wide_energy, mid)
    lhs = held(lhs)
    kinds = ((0, LANE_S), (0, LANE_R))
    places = (same_plane, high_plane)
    tot = correlate([tot], [lhs], kinds, [far(orbitals)], (0,), edge_plane, 6)

    edge_far = [hop(after(half, tot), INNER) for half in edge_pair]
    edge_next = hop(after(edge_inner, tot), OUTWARD)
    got = hop(give, INWARD)
    for pair, inner, where in zip(edge_pair, sides(edge_inner), places):
        tot = correlate([tot], [lhs], kinds, [pair, inner], (1, 2), where, 3)

    edge_last = [hop(after(edge_far[0], tot), OUTWARD), hop(after(edge_far[1], tot, edge_next), OUTWARD)]
    both = jnp.concatenate([mid, after(got, tot, *edge_far)[2 * count :]])
    both = hop(after(both, edge_next), INNER)
    mid_pair, mid_inner, mid_far = piece(got, bands, 2 * count // bands), piece(both, bands, 0), piece(both, bands, 1)
    mids = [mid, mid_pair, mid_inner, mid_far]
    for nearer, farther, where in zip(sides(edge_next), edge_far, places):
        tot = correlate([tot], [lhs], kinds, [nearer, farther], (2, 3), where, 3)
    given = correlate(
        [jnp.zeros((2 * count, 128), F32)], [piece(got, 2 * count, 0)], kinds,
        [mid, mid_inner, mid_far, mid_pair], (1, 2, 3, -100), same_plane, 2, True,
    )
    tot = correlate([tot], [lhs], kinds, mids, (0, 1, 2, 3), mid_plane, 2)
    taken = hop(after(given, tot), OUTWARD)
    tot = correlate([tot], [lhs], kinds, [edge_last[0]], (3,), same_plane, 3)

    lane = lax.iota(jnp.int32, 128)
    group = jnp.where(
        place < groups // 2,
        jnp.stack([place, 1 - place, jnp.int32(2), jnp.int32(3)]),
        jnp.stack([place, 5 - place, jnp.int32(1), jnp.int32(0)]),
    )
    ids = (group[:, None] * bands + lax.iota(jnp.int32, bands)[None, :]).reshape(used)
    cells = float(residual.shape[1] * lax.axis_size("grid") * residual.shape[2] * residual.shape[3])
    member = jnp.where(ids[None, :] // PB == panel_index[:, None], jnp.float32(1.0 / cells), jnp.float32(0.0))
    member = jnp.pad(member, ((0, 0), (0, 128 - used)), constant_values=1.0)
    inside = jnp.where(is_end, 0.0, 1.0)
    info = jnp.where(
        lane[None, :] == 0,
        old_product[:, None],
        jnp.where(lane[None, :] == 1, energy[:, None], inside),
    )
    cap = given * inside + taken
    tot, cap, info, member = lax.optimization_barrier((tot, cap, info, member))
    tot = correlate([tot, taken], [lhs], kinds, [edge_last[1]], (3,), high_plane, 3, False, member)
    tot = grid_sum(tot)

    slots = [
        [[halves[half]], [edge_pair[half]], [inner, nearer], [edge_far[half], edge_last[half]]]
        for half, inner, nearer in zip(range(2), sides(edge_inner), sides(edge_next))
    ]
    other_tot = hop(tot, INWARD)
    wide, low, *scalings = directions((tot, cap), info, start, direction, slots[0], 3, 3)
    from_right = lax.ppermute(low, "grid", downward)
    lost = removals(after(other_tot, low), cap, [[mid_pair], [mid], [mid_inner], [mid_far]], count)
    lost = (lost * jnp.float32(TOP)).astype(jnp.float16)
    wide, high = directions(scalings, after(info, lost), start, direction, slots[1], 3, 8, wide)
    from_left = lax.ppermute(high, "grid", upward)
    lost = hop(lost, OUTWARD).astype(F32) * jnp.float32(1.0 / TOP)
    (wide,) = directions(
        scalings, info, start, direction, [[m] for m in mids], 2, 6, wide, lost
    )
    new, image, curve, keep, _, residual, solution = images(
        info, from_left, wide, from_right, potential, residual, solution
    )
    curve = grid_sum(curve)
    new_solution, new_residual = finish(tot, info, curve, keep, image, residual, solution)
    return new_solution, new_residual, new, scalings[1][2, :, 0]


def solution(mesh):
    tiles = P("band", "grid", None, None)
    return jax.shard_map(
        on_device,
        mesh=mesh,
        in_specs=(tiles, tiles, tiles, P("band"), tiles, P(), P("grid", None, None), P("band"), P("band")),
        out_specs=(tiles, tiles, tiles, P("band")),
        check_vma=False,
    )
```

```python
import functools

import jax
import jax.numpy as jnp
from jax import lax
from jax.experimental import pallas as pl
from jax.experimental.pallas import tpu as pltpu
from jax.sharding import PartitionSpec as P

PB = 16
K0 = -49.0 / 18.0
SIDE = (270.0, -27.0, 2.0)
SCALE = -0.5 / 180.0
F32, BF16 = jnp.float32, jnp.bfloat16
TILE = 16
MIB = 1 << 20
TOP = 16384.0
NT = (((1,), (1,)), ((), ()))
LANE_S, LANE_R, LANE_RS, LANE_CAP = 0, 32, 96, 100


def edge_plane(i):
    return i + 2 * (i // 3)


def high_plane(i):
    return i + 5


def mid_plane(i):
    return i + 3


def same_plane(i):
    return i


def plane_spec(shape, place, part=0):
    return pl.BlockSpec((shape[0], 1) + tuple(shape[2:]), lambda i: (part, place(i), 0, 0))


def piece(array, size, part, first=0):
    return array, (size,) + tuple(array.shape[1:]), part, first


def as_piece(x):
    return x if isinstance(x, tuple) else piece(x, x.shape[0], 0)


def piece_spec(x, planes, place):
    array, shape, part, first = x
    return plane_spec(shape, place if shape[1] == planes else (lambda i: i + first), part)


def whole_spec(shape):
    return pl.BlockSpec(tuple(shape), lambda i: (0,) * len(shape))


def params(limit):
    return pltpu.CompilerParams(vmem_limit_bytes=limit * MIB)


CHEAP = pl.CostEstimate(flops=10**6, bytes_accessed=MIB, transcendentals=0)


DIRECT = pl.BlockSpec(memory_space=pltpu.VMEM)


def near(shape, dtype):
    return pltpu.VMEM(tuple(shape), dtype)


def far(x):
    return pltpu.with_memory_space_constraint(x, pltpu.HBM)


def held(x):
    return pltpu.with_memory_space_constraint(x, pltpu.VMEM)


def dot(a, b):
    return jnp.dot(a, b, preferred_element_type=F32)


def exact_dot(a, b):
    return jnp.dot(a, b, precision=lax.Precision.HIGHEST, preferred_element_type=F32)


def split(x):
    high = x.astype(BF16)
    return high, (x - high.astype(F32)).astype(BF16)


def in_lane(column, lane):
    at = lax.broadcasted_iota(jnp.int32, (column.shape[0], 128), 1)
    return jnp.where(at == lane, column, 0.0)


def prepare_kernel(planes, r_ref, d_ref, v_ref, e_ref, o_ref, s_ref, keep_ref, lhs_ref, give_ref, sum_ref, total):
    i = pl.program_id(0)
    count = r_ref.shape[0]

    @pl.when(i == 0)
    def _():
        total[...] = jnp.zeros_like(total)

    r = r_ref[:, 0]
    s = r / (v_ref[0][None] - e_ref[:, 0:1][:, :, None] - 1.5 * K0)
    s_ref[:, i] = s
    keep_ref[:, i] = d_ref[:, 0]
    short = s.astype(BF16)
    lhs_ref[:count, 0] = short
    lhs_ref[count:, 0] = r.astype(BF16)
    total[...] += jnp.sum(r * s, axis=1)

    @pl.when((i == planes // 2 - 1) | (i == planes // 2))
    def _():
        give_ref[:count, 0] = short
        give_ref[count : 2 * count, 0] = r.astype(BF16)
        give_ref[2 * count :] = o_ref[...]

    @pl.when(i == planes - 1)
    def _():
        sum_ref[:count] = jnp.zeros((count, 128), F32)
        sum_ref[count:] = in_lane(jnp.sum(total[...], axis=1, keepdims=True), LANE_RS)


def prepare(residual, direction, potential, energy, mid):
    shape = residual.shape
    count, planes, rows, depth = shape
    cut = lambda fields, size: (fields, size) + tuple(shape[2:])
    middle = lambda i: jnp.clip(i - 3, 0, 1)
    outs = [cut(2 * count, planes), cut(2 * count + mid.shape[0], 2)]
    maps = [same_plane, middle]
    return pl.pallas_call(
        functools.partial(prepare_kernel, planes),
        grid=(planes,),
        in_specs=[
            plane_spec(shape, same_plane),
            plane_spec(shape, same_plane),
            pl.BlockSpec((1, rows, depth), lambda i: (i, 0, 0)),
            whole_spec(energy.shape),
            plane_spec(mid.shape, middle),
        ],
        out_specs=[DIRECT] * 2 + [plane_spec(o, m) for o, m in zip(outs, maps)] + [whole_spec((2 * count, 128))],
        out_shape=[near(shape, F32)] * 2 + [near(o, BF16) for o in outs] + [jax.ShapeDtypeStruct((2 * count, 128), F32)],
        scratch_shapes=[pltpu.VMEM((count, depth), F32)],
        compiler_params=params(8),
        cost_estimate=CHEAP,
        name="prepare",
    )(far(residual), far(direction), far(potential), energy, mid)


def corr_kernel(slots, offsets, steps, lefts, arity, sums_in, capped, masked, *refs):
    prevs, refs = refs[:sums_in], refs[sums_in:]
    if masked:
        mask_ref, refs = refs[0], refs[1:]
    lhs, refs = refs[:lefts], refs[lefts:]
    terms, out_ref, acc, top = refs[:arity], refs[arity], refs[arity + 1], refs[arity + 2]
    i = pl.program_id(0)

    @pl.when(i == 0)
    def _():
        acc[...] = jnp.zeros_like(acc)
        top[...] = jnp.zeros_like(top)

    bands = terms[0].shape[0]
    rows, depth = terms[0].shape[2], terms[0].shape[3]
    for y in range(0, rows, TILE):
        at = lambda r: r[:, 0, y : y + TILE, :].reshape(r.shape[0] * TILE, depth)
        right = jnp.concatenate([at(t) for t in terms], axis=0)
        if capped:
            size = jnp.max(jnp.abs(right.astype(F32)), axis=0, keepdims=True)
            top[...] = jnp.maximum(top[...], jnp.broadcast_to(size, top.shape))
        row = 0
        for ref in lhs:
            size = ref.shape[0] * TILE
            acc[row : row + size, :] += lax.dot_general(at(ref), right, NT, preferred_element_type=F32)
            row += size

    @pl.when(i == steps - 1)
    def _():
        width = acc.shape[1]
        row = lax.broadcasted_iota(jnp.int32, acc.shape, 0)
        col = lax.broadcasted_iota(jnp.int32, acc.shape, 1)
        same = jnp.where((row & (TILE - 1)) == (col & (TILE - 1)), acc[...], 0.0)
        red = jnp.sum(same.reshape(acc.shape[0] // TILE, TILE, width), axis=1)
        src = lax.broadcasted_iota(jnp.int32, (width, 128), 0)
        dst = lax.broadcasted_iota(jnp.int32, (width, 128), 1)
        band = src // TILE
        goal = jnp.full_like(band, -1000)
        for number, slot in enumerate(slots):
            goal = jnp.where(band // bands == number, slot * bands + band % bands, goal)
        total = prevs[0][...]
        for prev in prevs[1:]:
            total = total + prev[...]
        out_ref[...] = total
        per = red.shape[0] // len(offsets)
        for number, (top_row, lane) in enumerate(offsets):
            place = jnp.where(goal + lane == dst, 1.0, 0.0).astype(F32)
            out_ref[top_row : top_row + per, :] += exact_dot(red[number * per : (number + 1) * per], place)
        if capped:
            most = jnp.max(top[...], axis=1, keepdims=True)
            out_ref[per : 2 * per, :] += in_lane(most, LANE_CAP)
        if masked:
            out_ref[:per, :] = out_ref[:per, :] * mask_ref[...]


def correlate(prevs, lhs, offsets, terms, slots, place, steps, capped=False, mask=None):
    lhs, terms = [as_piece(a) for a in lhs], [as_piece(t) for t in terms]
    spec = lambda a: piece_spec(a, 8, place)
    fields, bands = sum(a[1][0] for a in lhs), terms[0][1][0]
    small = list(prevs) + ([] if mask is None else [mask])
    return pl.pallas_call(
        functools.partial(
            corr_kernel, slots, offsets, steps, len(lhs), len(terms), len(prevs), capped, mask is not None
        ),
        grid=(steps,),
        in_specs=[whole_spec(p.shape) for p in small] + [spec(a) for a in [*lhs, *terms]],
        out_specs=whole_spec(prevs[0].shape),
        out_shape=jax.ShapeDtypeStruct(prevs[0].shape, F32),
        scratch_shapes=[
            pltpu.VMEM((fields * TILE, len(terms) * bands * TILE), F32),
            pltpu.VMEM((8, terms[0][1][3]), F32),
        ],
        compiler_params=params(10),
        cost_estimate=CHEAP,
        name="correlate",
    )(*small, *[a[0] for a in lhs], *[t[0] for t in terms])


def band_matrix(size, period):
    row = lax.broadcasted_iota(jnp.int32, (size, size), 0)
    col = lax.broadcasted_iota(jnp.int32, (size, size), 1)
    away = jnp.abs(row - col)
    value = jnp.where(away == 1, SIDE[0], jnp.where(away == 2, SIDE[1], jnp.where(away == 3, SIDE[2], 0.0)))
    return jnp.where(row // period == col // period, value, 0.0).astype(BF16)


def coefficients(tot_ref, count):
    lane = lax.broadcasted_iota(jnp.int32, (count, 128), 1)
    return jnp.where(lane < LANE_R, tot_ref[:count], 0.0)


def scalars(tot_ref, info_ref):
    count = info_ref.shape[0]
    raw = tot_ref[:count, LANE_S : LANE_S + 32]
    product = tot_ref[count : 2 * count, LANE_RS : LANE_RS + 1]
    product = product - jnp.sum(raw * tot_ref[:count, LANE_R : LANE_R + 32], axis=1, keepdims=True)
    return product, product / info_ref[:, 0:1]


def widened(chosen, w_ref):
    count, width = chosen.shape[0], w_ref.shape[1]
    src = lax.broadcasted_iota(jnp.int32, (128, width), 0)
    dst = lax.broadcasted_iota(jnp.int32, (128, width), 1)
    spread = jnp.where(src == dst // TILE, 1.0, 0.0).astype(BF16)
    row = lax.broadcasted_iota(jnp.int32, (count, TILE, width), 1)
    col = lax.broadcasted_iota(jnp.int32, (count, TILE, width), 2)
    for half, part in enumerate(split(chosen)):
        wide = jnp.broadcast_to(dot(part, spread)[:, None, :], (count, TILE, width))
        kron = jnp.where(row == (col & (TILE - 1)), wide, 0.0)
        w_ref[half * count * TILE : (half + 1) * count * TILE, :] = kron.reshape(
            count * TILE, width
        ).astype(BF16)


def combined(w_ref, groups, plane, y):
    every = []
    for group in groups:
        parts = [
            ref[size * part : size * (part + 1), plane + first, y : y + TILE, :] for ref, size, part, first in group
        ]
        whole = parts[0]
        for part in parts[1:]:
            whole = whole + part
        every.append(whole.reshape(whole.shape[0] * TILE, whole.shape[2]))
    both = dot(w_ref[...], jnp.concatenate(every, axis=0))
    half = both.shape[0] // 2
    return (both[:half] + both[half:]).reshape(half // TILE, TILE, both.shape[1])


def grouped(refs, layout):
    groups, at = [], 0
    for group in layout:
        groups.append([(refs[at + number], *where) for number, where in enumerate(group)])
        at += len(group)
    return groups, refs[at:]


def laid_out(slots):
    flat = [as_piece(o) for group in slots for o in group]
    layout, at = [], 0
    for group in slots:
        layout.append([(o[1][0], o[2], o[3]) for o in flat[at : at + len(group)]])
        at += len(group)
    return [held(o[0]) for o in flat], layout


def direction_kernel(layout, first, edges, base, aliased, *refs):
    if first:
        (tot_ref, info_ref, cap_ref), refs = refs[:3], refs[3:]
    else:
        (info_ref, w_ref, scale_ref), refs = refs[:3], refs[3:]
    (s_ref, d_ref), rest = refs[:2], refs[2:]
    groups, rest = grouped(rest, layout)
    if not edges:
        lost_ref, rest = rest[0], rest[1:]
    n_ref, rest = rest[aliased], rest[aliased + 1 :]
    if edges:
        side_ref, rest = rest[0], rest[1:]
    i = pl.program_id(0)
    count = info_ref.shape[0]

    if first:
        w_ref, scale_ref = rest

        @pl.when(i == 0)
        def _():
            product, beta = scalars(tot_ref, info_ref)
            chosen = coefficients(tot_ref, count)
            for number, column in enumerate((beta, reach(chosen, cap_ref), product)):
                scale_ref[number] = jnp.broadcast_to(column, scale_ref.shape[1:])
            widened(chosen, w_ref)

    beta = scale_ref[0][:, 0:1][:, :, None]
    for y in range(0, s_ref.shape[2], TILE):
        part = slice(y, y + TILE)
        removed = combined(w_ref, groups, i, y)
        if not edges:
            removed = info_ref[:, 2:3][:, :, None] * removed
            removed = removed + scale_ref[1][:, 0:1][:, :, None] * lost_ref[:, 0, part, :]
        new = s_ref[:, base - 3 + i, part, :] - removed + beta * d_ref[:, base - 3 + i, part, :]
        if edges:
            side_ref[:, 0, part, :] = new.astype(BF16)
        n_ref[:, base + i, part, :] = new


def directions(scalings, info, start, direction, slots, steps, base, so_far=None, lost=None):
    shape = start.shape
    first, edges = so_far is None, lost is None
    wide = (shape[0], shape[1] + 6) + tuple(shape[2:])
    part = (shape[0], steps) + tuple(shape[2:])
    flat, layout = laid_out(slots)
    if first:
        tot, cap = scalings
        args = [tot, info, cap]
        in_specs = [whole_spec(a.shape) for a in args]
    else:
        args = [info, held(scalings[0]), held(scalings[1])]
        in_specs = [whole_spec(info.shape), DIRECT, DIRECT]
    args += [held(start), held(direction), *flat]
    in_specs += [DIRECT] * (2 + len(flat))
    if not edges:
        args.append(lost)
        in_specs.append(plane_spec(part, same_plane))
    aliases = {}
    if not first:
        aliases = {len(args): 0}
        args.append(held(so_far))
        in_specs.append(DIRECT)
    out_specs, out_shape = [DIRECT], [near(wide, F32)]
    if edges:
        out_specs.append(plane_spec(part, same_plane))
        out_shape.append(near(part, BF16))
    if first:
        out_specs += [DIRECT, DIRECT]
        out_shape += [
            near((2 * shape[0] * TILE, len(slots) * layout[0][0][0] * TILE), BF16),
            near((3, shape[0], 128), F32),
        ]
    work = 3 if edges else 64
    return pl.pallas_call(
        functools.partial(direction_kernel, layout, first, edges, base, len(aliases)),
        grid=(steps,),
        in_specs=in_specs,
        out_specs=out_specs,
        out_shape=out_shape,
        input_output_aliases=aliases,
        compiler_params=params(6),
        cost_estimate=pl.CostEstimate(
            flops=steps * 2 * 256 * 1024 * 384, bytes_accessed=work * MIB, transcendentals=0
        ),
        name="directions",
    )(*args)


def reach(chosen, cap_ref):
    count = chosen.shape[0]
    cap = cap_ref[count : 2 * count, LANE_CAP : LANE_CAP + 1]
    return jnp.maximum(jnp.sum(jnp.abs(chosen), axis=1, keepdims=True) * cap, 1e-30)


def removal_kernel(layout, flag_ref, tot_ref, cap_ref, *rest):
    groups, (out_ref, w_ref) = grouped(rest, layout)

    @pl.when((pl.program_id(0) == 0) & (flag_ref[0] > 0))
    def _():
        chosen = coefficients(tot_ref, out_ref.shape[0])
        widened(chosen / reach(chosen, cap_ref), w_ref)

    @pl.when(flag_ref[0] > 0)
    def _():
        for y in range(0, out_ref.shape[2], TILE):
            out_ref[:, 0, y : y + TILE, :] = combined(w_ref, groups, pl.program_id(0), y)

    @pl.when(flag_ref[0] == 0)
    def _():
        out_ref[...] = jnp.zeros_like(out_ref)


def removals(flag, tot, cap, slots, count):
    flat, layout = laid_out(slots)
    shape = (count,) + tuple(as_piece(slots[0][0])[1][1:])
    return pl.pallas_call(
        functools.partial(removal_kernel, layout),
        grid=(shape[1],),
        in_specs=[pl.BlockSpec(memory_space=pltpu.SMEM), whole_spec(tot.shape), whole_spec(cap.shape)]
        + [DIRECT] * len(flat),
        out_specs=plane_spec(shape, same_plane),
        out_shape=near(shape, F32),
        scratch_shapes=[
            pltpu.VMEM((2 * count * TILE, len(slots) * layout[0][0][0] * TILE), BF16),
        ],
        compiler_params=params(6),
        cost_estimate=pl.CostEstimate(
            flops=2 * 2 * 256 * 1024 * 384, bytes_accessed=4 * MIB, transcendentals=0
        ),
        name="removals",
    )(flag, tot, cap, *flat)


def image_kernel(
    planes, info_ref, low_ref, high_ref, v_ref, wide_in, r_ref, x_ref,
    new_ref, image_ref, curve_ref, keep_ref, n_ref, r_near, x_near, ky, kz, even, odd, total, sem,
):
    i = pl.program_id(0)
    count, _, rows, depth = n_ref.shape

    @pl.when(i == 0)
    def _():
        ky[...] = band_matrix(count * rows, rows)
        kz[...] = band_matrix(depth, depth)
        total[...] = jnp.zeros_like(total)
        pltpu.make_async_copy(r_ref, r_near, sem.at[0]).start()
        pltpu.make_async_copy(x_ref, x_near, sem.at[1]).start()
        n_ref[:, 0:3] = low_ref[...].astype(F32)
        n_ref[:, planes + 3 : planes + 6] = high_ref[...].astype(F32)

    for half, beside in enumerate((even, odd)):
        high, low = split(n_ref[:, 2 * i + half + 3].reshape(count * rows, depth))
        sides = dot(ky[...], high) + dot(ky[...], low) + dot(high, kz[...]) + dot(low, kz[...])
        beside[...] = sides.reshape(beside.shape)
    for half, beside in enumerate((even, odd)):
        plane = 2 * i + half + 3
        shifted = v_ref[half] - 1.5 * K0
        for c in range(count):
            here = n_ref[c, plane]
            side = beside[c]
            for away in range(1, 4):
                side = side + SIDE[away - 1] * (n_ref[c, plane - away] + n_ref[c, plane + away])
            image = SCALE * side + (shifted - info_ref[c : c + 1, 1:2]) * here
            new_ref[c, half] = here
            keep_ref[c, plane - 3] = here
            image_ref[c, plane - 3] = image
            total[c : c + 1] += jnp.sum(here * image, axis=0, keepdims=True)

    @pl.when(i == planes // 2 - 1)
    def _():
        curve_ref[...] = jnp.broadcast_to(jnp.sum(total[...], axis=1, keepdims=True), curve_ref.shape)
        pltpu.make_async_copy(r_ref, r_near, sem.at[0]).wait()
        pltpu.make_async_copy(x_ref, x_near, sem.at[1]).wait()


def images(info, low, wide, high, potential, residual, solution):
    count, _, rows, depth = wide.shape
    planes = potential.shape[0]
    shape = (count, planes, rows, depth)
    return pl.pallas_call(
        functools.partial(image_kernel, planes),
        grid=(planes // 2,),
        in_specs=[
            whole_spec(info.shape), DIRECT, DIRECT,
            pl.BlockSpec((2, rows, depth), lambda i: (i, 0, 0)),
            DIRECT,
        ]
        + [pl.BlockSpec(memory_space=pl.ANY)] * 2,
        out_specs=[
            pl.BlockSpec((count, 2, rows, depth), lambda i: (0, i, 0, 0)), DIRECT, whole_spec((count, 128)),
        ]
        + [DIRECT] * 4,
        out_shape=[
            pltpu.HBM(shape, F32), near(shape, F32), jax.ShapeDtypeStruct((count, 128), F32),
            near(shape, F32), near(wide.shape, F32), near(shape, F32), near(shape, F32),
        ],
        input_output_aliases={4: 4},
        scratch_shapes=[
            pltpu.VMEM((count * rows, count * rows), BF16),
            pltpu.VMEM((depth, depth), BF16),
            pltpu.VMEM((count, rows, depth), F32),
            pltpu.VMEM((count, rows, depth), F32),
            pltpu.VMEM((count, depth), F32),
            pltpu.SemaphoreType.DMA((2,)),
        ],
        compiler_params=params(8),
        cost_estimate=pl.CostEstimate(flops=4 * 10**9, bytes_accessed=24 * MIB, transcendentals=0),
        name="images",
    )(info, held(low), held(high), far(potential), held(wide), far(residual), far(solution))


def finish_kernel(planes, tot_ref, info_ref, curve_ref, n_ref, image_ref, r_ref, x_ref, sol_ref, res_ref, sol, res, sem):
    product, _ = scalars(tot_ref, info_ref)
    size = jnp.broadcast_to(product / curve_ref[:, 0:1], info_ref.shape)[:, 0:1][:, :, None]
    copies = []
    for plane in range(planes):
        sol[:, plane] = x_ref[:, plane] + size * n_ref[:, plane]
        res[:, plane] = r_ref[:, plane] - size * image_ref[:, plane]
        for number, (source, target) in enumerate(((sol, sol_ref), (res, res_ref))):
            copy = pltpu.make_async_copy(source.at[:, plane], target.at[:, plane], sem.at[number, plane])
            copy.start()
            copies.append(copy)
    for copy in copies:
        copy.wait()


def finish(tot, info, curve, new, image, residual, solution):
    shape = new.shape
    return pl.pallas_call(
        functools.partial(finish_kernel, shape[1]),
        in_specs=[DIRECT] * 7,
        out_specs=[pl.BlockSpec(memory_space=pl.ANY)] * 2,
        out_shape=[pltpu.HBM(shape, F32)] * 2,
        scratch_shapes=[pltpu.VMEM(shape, F32)] * 2 + [pltpu.SemaphoreType.DMA((2, shape[1]))],
        compiler_params=params(8),
        name="finish",
    )(tot, info, curve, held(new), held(image), held(residual), held(solution))


def after(value, *others):
    return lax.optimization_barrier((value, *others))[0]


SWAP = [(0, 1), (1, 0), (2, 3), (3, 2)]
INNER = [(1, 2), (2, 1)]
INWARD = [(0, 1), (3, 2)]
OUTWARD = [(1, 0), (2, 3)]


def grid_sum(value):
    size = lax.axis_size("grid")
    away = lambda x, step: lax.ppermute(x, "grid", [(i, i ^ step) for i in range(size)])
    value = value + away(value, 1)
    stride = 2
    while stride < size:
        if 4 * stride <= size:
            near_by, above, across = (away(value, step * stride) for step in (1, 2, 3))
            value = (value + near_by) + (above + across)
            stride *= 4
        else:
            value = value + away(value, stride)
            stride *= 2
    return value


def hop(value, pairs):
    return lax.ppermute(value, "band", pairs)


def on_device(
    residual,
    direction,
    solution,
    old_product,
    orbitals,
    energies,
    potential,
    column_index,
    panel_index,
):
    count = residual.shape[0]
    bands = orbitals.shape[0]
    groups = lax.axis_size("band")
    place = lax.axis_index("band")
    is_end = (place == 0) | (place == groups - 1)
    ends = lax.axis_size("grid") - 1
    upward = [(i, i + 1) for i in range(ends)]
    downward = [(i + 1, i) for i in range(ends)]
    used = groups * bands

    halves = (orbitals[:, 0:3], orbitals[:, 5:8])
    mid = orbitals[:, 3:5]
    edge_pair = [hop(half, SWAP) for half in halves]
    edge_inner = hop(jnp.concatenate(halves, axis=1), INNER)
    sides = lambda x: [piece(x, bands, 0, 0), piece(x, bands, 0, 3)]

    band_ids = lax.iota(jnp.int32, energies.shape[0])
    picked = jnp.where(
        band_ids[None, :] == (column_index // 3)[:, None], energies[None, :], jnp.float32(0.0)
    )
    energy = jnp.sum(picked, axis=1)
    wide_energy = jnp.broadcast_to(energy[:, None], (count, 128))
    start, direction, lhs, give, tot = prepare(residual, direction, potential, wide_energy, mid)
    lhs = held(lhs)
    kinds = ((0, LANE_S), (0, LANE_R))
    places = (same_plane, high_plane)
    tot = correlate([tot], [lhs], kinds, [far(orbitals)], (0,), edge_plane, 6)

    edge_far = [hop(after(half, tot), INNER) for half in edge_pair]
    edge_next = hop(after(edge_inner, tot), OUTWARD)
    got = hop(give, INWARD)
    for pair, inner, where in zip(edge_pair, sides(edge_inner), places):
        tot = correlate([tot], [lhs], kinds, [pair, inner], (1, 2), where, 3)

    edge_last = [hop(after(edge_far[0], tot), OUTWARD), hop(after(edge_far[1], tot, edge_next), OUTWARD)]
    both = jnp.concatenate([mid, after(got, tot, *edge_far)[2 * count :]])
    both = hop(after(both, edge_next), INNER)
    mid_pair, mid_inner, mid_far = piece(got, bands, 2 * count // bands), piece(both, bands, 0), piece(both, bands, 1)
    mids = [mid, mid_pair, mid_inner, mid_far]
    for nearer, farther, where in zip(sides(edge_next), edge_far, places):
        tot = correlate([tot], [lhs], kinds, [nearer, farther], (2, 3), where, 3)
    given = correlate(
        [jnp.zeros((2 * count, 128), F32)], [piece(got, 2 * count, 0)], kinds,
        [mid, mid_inner, mid_far, mid_pair], (1, 2, 3, -100), same_plane, 2, True,
    )
    tot = correlate([tot], [lhs], kinds, mids, (0, 1, 2, 3), mid_plane, 2)
    taken = hop(after(given, tot), OUTWARD)
    tot = correlate([tot], [lhs], kinds, [held(edge_last[0])], (3,), same_plane, 3)

    lane = lax.iota(jnp.int32, 128)
    group = jnp.where(
        place < groups // 2,
        jnp.stack([place, 1 - place, jnp.int32(2), jnp.int32(3)]),
        jnp.stack([place, 5 - place, jnp.int32(1), jnp.int32(0)]),
    )
    ids = (group[:, None] * bands + lax.iota(jnp.int32, bands)[None, :]).reshape(used)
    cells = float(residual.shape[1] * lax.axis_size("grid") * residual.shape[2] * residual.shape[3])
    member = jnp.where(ids[None, :] // PB == panel_index[:, None], jnp.float32(1.0 / cells), jnp.float32(0.0))
    member = jnp.pad(member, ((0, 0), (0, 128 - used)), constant_values=1.0)
    inside = jnp.where(is_end, 0.0, 1.0)
    info = jnp.where(
        lane[None, :] == 0,
        old_product[:, None],
        jnp.where(lane[None, :] == 1, energy[:, None], inside),
    )
    cap = given * inside + taken
    flag = jnp.where(is_end, 0, 1).astype(jnp.int32).reshape(1)
    tot, cap, info, member, flag = lax.optimization_barrier((tot, cap, info, member, flag))
    tot = correlate([tot, taken], [lhs], kinds, [held(edge_last[1])], (3,), high_plane, 3, False, member)
    tot = grid_sum(tot)

    slots = [
        [[halves[half]], [edge_pair[half]], [inner, nearer], [edge_far[half], edge_last[half]]]
        for half, inner, nearer in zip(range(2), sides(edge_inner), sides(edge_next))
    ]
    other_tot = hop(tot, INWARD)
    wide, low, *scalings = directions((tot, cap), info, start, direction, slots[0], 3, 3)
    from_right = lax.ppermute(low, "grid", downward)
    lost = removals(flag, after(other_tot, low), cap, [[mid_pair], [mid], [mid_inner], [mid_far]], count)
    lost = (lost * jnp.float32(TOP)).astype(jnp.float16)
    wide, high = directions(scalings, after(info, lost), start, direction, slots[1], 3, 8, wide)
    from_left = lax.ppermute(high, "grid", upward)
    lost = hop(lost, OUTWARD).astype(F32) * jnp.float32(1.0 / TOP)
    (wide,) = directions(
        scalings, info, start, direction, [[m] for m in mids], 2, 6, wide, lost
    )
    new, image, curve, keep, _, residual, solution = images(
        info, from_left, wide, from_right, potential, residual, solution
    )
    curve = grid_sum(curve)
    new_solution, new_residual = finish(tot, info, curve, keep, image, residual, solution)
    return new_solution, new_residual, new, scalings[1][2, :, 0]


def solution(mesh):
    tiles = P("band", "grid", None, None)
    return jax.shard_map(
        on_device,
        mesh=mesh,
        in_specs=(tiles, tiles, tiles, P("band"), tiles, P(), P("grid", None, None), P("band"), P("band")),
        out_specs=(tiles, tiles, tiles, P("band")),
        check_vma=False,
    )
```

```python
import functools

import jax
import jax.numpy as jnp
from jax import lax
from jax.experimental import pallas as pl
from jax.experimental.pallas import tpu as pltpu
from jax.sharding import PartitionSpec as P

PB = 16
K0 = -49.0 / 18.0
SIDE = (270.0, -27.0, 2.0)
SCALE = -0.5 / 180.0
F32, BF16 = jnp.float32, jnp.bfloat16
TILE = 16
MIB = 1 << 20
TOP = 16384.0
NT = (((1,), (1,)), ((), ()))
LANE_S, LANE_R, LANE_RS, LANE_CAP = 0, 32, 96, 100


def edge_plane(i):
    return i + 2 * (i // 3)


def high_plane(i):
    return i + 5


def mid_plane(i):
    return i + 3


def same_plane(i):
    return i


def plane_spec(shape, place, part=0):
    return pl.BlockSpec((shape[0], 1) + tuple(shape[2:]), lambda i: (part, place(i), 0, 0))


def piece(array, size, part, first=0):
    return array, (size,) + tuple(array.shape[1:]), part, first


def as_piece(x):
    return x if isinstance(x, tuple) else piece(x, x.shape[0], 0)


def piece_spec(x, planes, place):
    array, shape, part, first = x
    return plane_spec(shape, place if shape[1] == planes else (lambda i: i + first), part)


def whole_spec(shape):
    return pl.BlockSpec(tuple(shape), lambda i: (0,) * len(shape))


def params(limit):
    return pltpu.CompilerParams(vmem_limit_bytes=limit * MIB)


CHEAP = pl.CostEstimate(flops=10**6, bytes_accessed=MIB, transcendentals=0)


DIRECT = pl.BlockSpec(memory_space=pltpu.VMEM)


def near(shape, dtype):
    return pltpu.VMEM(tuple(shape), dtype)


def far(x):
    return pltpu.with_memory_space_constraint(x, pltpu.HBM)


def held(x):
    return pltpu.with_memory_space_constraint(x, pltpu.VMEM)


def dot(a, b):
    return jnp.dot(a, b, preferred_element_type=F32)


def exact_dot(a, b):
    return jnp.dot(a, b, precision=lax.Precision.HIGHEST, preferred_element_type=F32)


def split(x):
    high = x.astype(BF16)
    return high, (x - high.astype(F32)).astype(BF16)


def in_lane(column, lane):
    at = lax.broadcasted_iota(jnp.int32, (column.shape[0], 128), 1)
    return jnp.where(at == lane, column, 0.0)


def prepare_kernel(planes, r_ref, d_ref, v_ref, e_ref, o_ref, s_ref, keep_ref, lhs_ref, give_ref, sum_ref, total):
    i = pl.program_id(0)
    count = r_ref.shape[0]

    @pl.when(i == 0)
    def _():
        total[...] = jnp.zeros_like(total)

    r = r_ref[:, 0]
    s = r / (v_ref[0][None] - e_ref[:, 0:1][:, :, None] - 1.5 * K0)
    s_ref[:, i] = s
    keep_ref[:, i] = d_ref[:, 0]
    short = s.astype(BF16)
    lhs_ref[:count, 0] = short
    lhs_ref[count:, 0] = r.astype(BF16)
    total[...] += jnp.sum(r * s, axis=1)

    @pl.when((i == planes // 2 - 1) | (i == planes // 2))
    def _():
        give_ref[:count, 0] = short
        give_ref[count : 2 * count, 0] = r.astype(BF16)
        give_ref[2 * count :] = o_ref[...]

    @pl.when(i == planes - 1)
    def _():
        sum_ref[:count] = jnp.zeros((count, 128), F32)
        sum_ref[count:] = in_lane(jnp.sum(total[...], axis=1, keepdims=True), LANE_RS)


def prepare(residual, direction, potential, energy, mid):
    shape = residual.shape
    count, planes, rows, depth = shape
    cut = lambda fields, size: (fields, size) + tuple(shape[2:])
    middle = lambda i: jnp.clip(i - 3, 0, 1)
    outs = [cut(2 * count, planes), cut(2 * count + mid.shape[0], 2)]
    maps = [same_plane, middle]
    return pl.pallas_call(
        functools.partial(prepare_kernel, planes),
        grid=(planes,),
        in_specs=[
            plane_spec(shape, same_plane),
            plane_spec(shape, same_plane),
            pl.BlockSpec((1, rows, depth), lambda i: (i, 0, 0)),
            whole_spec(energy.shape),
            plane_spec(mid.shape, middle),
        ],
        out_specs=[DIRECT] * 2 + [plane_spec(o, m) for o, m in zip(outs, maps)] + [whole_spec((2 * count, 128))],
        out_shape=[near(shape, F32)] * 2 + [near(o, BF16) for o in outs] + [jax.ShapeDtypeStruct((2 * count, 128), F32)],
        scratch_shapes=[pltpu.VMEM((count, depth), F32)],
        compiler_params=params(8),
        cost_estimate=CHEAP,
        name="prepare",
    )(far(residual), far(direction), far(potential), energy, mid)


def corr_kernel(slots, offsets, steps, lefts, arity, sums_in, capped, masked, *refs):
    prevs, refs = refs[:sums_in], refs[sums_in:]
    if masked:
        mask_ref, refs = refs[0], refs[1:]
    lhs, refs = refs[:lefts], refs[lefts:]
    terms, out_ref, acc, top = refs[:arity], refs[arity], refs[arity + 1], refs[arity + 2]
    i = pl.program_id(0)

    @pl.when(i == 0)
    def _():
        acc[...] = jnp.zeros_like(acc)
        top[...] = jnp.zeros_like(top)

    bands = terms[0].shape[0]
    rows, depth = terms[0].shape[2], terms[0].shape[3]
    for y in range(0, rows, TILE):
        at = lambda r: r[:, 0, y : y + TILE, :].reshape(r.shape[0] * TILE, depth)
        right = jnp.concatenate([at(t) for t in terms], axis=0)
        if capped:
            size = jnp.max(jnp.abs(right.astype(F32)), axis=0, keepdims=True)
            top[...] = jnp.maximum(top[...], jnp.broadcast_to(size, top.shape))
        row = 0
        for ref in lhs:
            size = ref.shape[0] * TILE
            acc[row : row + size, :] += lax.dot_general(at(ref), right, NT, preferred_element_type=F32)
            row += size

    @pl.when(i == steps - 1)
    def _():
        width = acc.shape[1]
        row = lax.broadcasted_iota(jnp.int32, acc.shape, 0)
        col = lax.broadcasted_iota(jnp.int32, acc.shape, 1)
        same = jnp.where((row & (TILE - 1)) == (col & (TILE - 1)), acc[...], 0.0)
        red = jnp.sum(same.reshape(acc.shape[0] // TILE, TILE, width), axis=1)
        src = lax.broadcasted_iota(jnp.int32, (width, 128), 0)
        dst = lax.broadcasted_iota(jnp.int32, (width, 128), 1)
        band = src // TILE
        goal = jnp.full_like(band, -1000)
        for number, slot in enumerate(slots):
            goal = jnp.where(band // bands == number, slot * bands + band % bands, goal)
        total = prevs[0][...]
        for prev in prevs[1:]:
            total = total + prev[...]
        out_ref[...] = total
        per = red.shape[0] // len(offsets)
        for number, (top_row, lane) in enumerate(offsets):
            place = jnp.where(goal + lane == dst, 1.0, 0.0).astype(F32)
            out_ref[top_row : top_row + per, :] += exact_dot(red[number * per : (number + 1) * per], place)
        if capped:
            most = jnp.max(top[...], axis=1, keepdims=True)
            out_ref[per : 2 * per, :] += in_lane(most, LANE_CAP)
        if masked:
            out_ref[:per, :] = out_ref[:per, :] * mask_ref[...]


def correlate(prevs, lhs, offsets, terms, slots, place, steps, capped=False, mask=None):
    lhs, terms = [as_piece(a) for a in lhs], [as_piece(t) for t in terms]
    spec = lambda a: piece_spec(a, 8, place)
    fields, bands = sum(a[1][0] for a in lhs), terms[0][1][0]
    small = list(prevs) + ([] if mask is None else [mask])
    return pl.pallas_call(
        functools.partial(
            corr_kernel, slots, offsets, steps, len(lhs), len(terms), len(prevs), capped, mask is not None
        ),
        grid=(steps,),
        in_specs=[whole_spec(p.shape) for p in small] + [spec(a) for a in [*lhs, *terms]],
        out_specs=whole_spec(prevs[0].shape),
        out_shape=jax.ShapeDtypeStruct(prevs[0].shape, F32),
        scratch_shapes=[
            pltpu.VMEM((fields * TILE, len(terms) * bands * TILE), F32),
            pltpu.VMEM((8, terms[0][1][3]), F32),
        ],
        compiler_params=params(10),
        cost_estimate=CHEAP,
        name="correlate",
    )(*small, *[a[0] for a in lhs], *[t[0] for t in terms])


def band_matrix(size, period):
    row = lax.broadcasted_iota(jnp.int32, (size, size), 0)
    col = lax.broadcasted_iota(jnp.int32, (size, size), 1)
    away = jnp.abs(row - col)
    value = jnp.where(away == 1, SIDE[0], jnp.where(away == 2, SIDE[1], jnp.where(away == 3, SIDE[2], 0.0)))
    return jnp.where(row // period == col // period, value, 0.0).astype(BF16)


def coefficients(tot_ref, count):
    lane = lax.broadcasted_iota(jnp.int32, (count, 128), 1)
    return jnp.where(lane < LANE_R, tot_ref[:count], 0.0)


def scalars(tot_ref, info_ref):
    count = info_ref.shape[0]
    raw = tot_ref[:count, LANE_S : LANE_S + 32]
    product = tot_ref[count : 2 * count, LANE_RS : LANE_RS + 1]
    product = product - jnp.sum(raw * tot_ref[:count, LANE_R : LANE_R + 32], axis=1, keepdims=True)
    return product, product / info_ref[:, 0:1]


def widened(chosen, w_ref):
    count, width = chosen.shape[0], w_ref.shape[1]
    src = lax.broadcasted_iota(jnp.int32, (128, width), 0)
    dst = lax.broadcasted_iota(jnp.int32, (128, width), 1)
    spread = jnp.where(src == dst // TILE, 1.0, 0.0).astype(BF16)
    row = lax.broadcasted_iota(jnp.int32, (count, TILE, width), 1)
    col = lax.broadcasted_iota(jnp.int32, (count, TILE, width), 2)
    for half, part in enumerate(split(chosen)):
        wide = jnp.broadcast_to(dot(part, spread)[:, None, :], (count, TILE, width))
        kron = jnp.where(row == (col & (TILE - 1)), wide, 0.0)
        w_ref[half * count * TILE : (half + 1) * count * TILE, :] = kron.reshape(
            count * TILE, width
        ).astype(BF16)


def combined(w_ref, groups, plane, y):
    every = []
    for group in groups:
        parts = [
            ref[size * part : size * (part + 1), plane + first, y : y + TILE, :] for ref, size, part, first in group
        ]
        whole = parts[0]
        for part in parts[1:]:
            whole = whole + part
        every.append(whole.reshape(whole.shape[0] * TILE, whole.shape[2]))
    both = dot(w_ref[...], jnp.concatenate(every, axis=0))
    half = both.shape[0] // 2
    return (both[:half] + both[half:]).reshape(half // TILE, TILE, both.shape[1])


def grouped(refs, layout):
    groups, at = [], 0
    for group in layout:
        groups.append([(refs[at + number], *where) for number, where in enumerate(group)])
        at += len(group)
    return groups, refs[at:]


def laid_out(slots):
    flat = [as_piece(o) for group in slots for o in group]
    layout, at = [], 0
    for group in slots:
        layout.append([(o[1][0], o[2], o[3]) for o in flat[at : at + len(group)]])
        at += len(group)
    return [held(o[0]) for o in flat], layout


def direction_kernel(layout, first, edges, base, aliased, *refs):
    if first:
        (tot_ref, info_ref, cap_ref), refs = refs[:3], refs[3:]
    else:
        (info_ref, w_ref, scale_ref), refs = refs[:3], refs[3:]
    (s_ref, d_ref), rest = refs[:2], refs[2:]
    groups, rest = grouped(rest, layout)
    if not edges:
        lost_ref, rest = rest[0], rest[1:]
    n_ref, rest = rest[aliased], rest[aliased + 1 :]
    if edges:
        side_ref, rest = rest[0], rest[1:]
    i = pl.program_id(0)
    count = info_ref.shape[0]

    if first:
        w_ref, scale_ref = rest

        @pl.when(i == 0)
        def _():
            product, beta = scalars(tot_ref, info_ref)
            chosen = coefficients(tot_ref, count)
            for number, column in enumerate((beta, reach(chosen, cap_ref), product)):
                scale_ref[number] = jnp.broadcast_to(column, scale_ref.shape[1:])
            widened(chosen, w_ref)

    beta = scale_ref[0][:, 0:1][:, :, None]
    for y in range(0, s_ref.shape[2], TILE):
        part = slice(y, y + TILE)
        removed = combined(w_ref, groups, i, y)
        if not edges:
            removed = info_ref[:, 2:3][:, :, None] * removed
            removed = removed + scale_ref[1][:, 0:1][:, :, None] * lost_ref[:, 0, part, :]
        new = s_ref[:, base - 3 + i, part, :] - removed + beta * d_ref[:, base - 3 + i, part, :]
        if edges:
            side_ref[:, 0, part, :] = new.astype(BF16)
        n_ref[:, base + i, part, :] = new


def directions(scalings, info, start, direction, slots, steps, base, so_far=None, lost=None):
    shape = start.shape
    first, edges = so_far is None, lost is None
    wide = (shape[0], shape[1] + 6) + tuple(shape[2:])
    part = (shape[0], steps) + tuple(shape[2:])
    flat, layout = laid_out(slots)
    if first:
        tot, cap = scalings
        args = [tot, info, cap]
        in_specs = [whole_spec(a.shape) for a in args]
    else:
        args = [info, held(scalings[0]), held(scalings[1])]
        in_specs = [whole_spec(info.shape), DIRECT, DIRECT]
    args += [held(start), held(direction), *flat]
    in_specs += [DIRECT] * (2 + len(flat))
    if not edges:
        args.append(lost)
        in_specs.append(plane_spec(part, same_plane))
    aliases = {}
    if not first:
        aliases = {len(args): 0}
        args.append(held(so_far))
        in_specs.append(DIRECT)
    out_specs, out_shape = [DIRECT], [near(wide, F32)]
    if edges:
        out_specs.append(plane_spec(part, same_plane))
        out_shape.append(near(part, BF16))
    if first:
        out_specs += [DIRECT, DIRECT]
        out_shape += [
            near((2 * shape[0] * TILE, len(slots) * layout[0][0][0] * TILE), BF16),
            near((3, shape[0], 128), F32),
        ]
    work = 3 if edges else 64
    return pl.pallas_call(
        functools.partial(direction_kernel, layout, first, edges, base, len(aliases)),
        grid=(steps,),
        in_specs=in_specs,
        out_specs=out_specs,
        out_shape=out_shape,
        input_output_aliases=aliases,
        compiler_params=params(6),
        cost_estimate=pl.CostEstimate(
            flops=steps * 2 * 256 * 1024 * 384, bytes_accessed=work * MIB, transcendentals=0
        ),
        name="directions",
    )(*args)


def reach(chosen, cap_ref):
    count = chosen.shape[0]
    cap = cap_ref[count : 2 * count, LANE_CAP : LANE_CAP + 1]
    return jnp.maximum(jnp.sum(jnp.abs(chosen), axis=1, keepdims=True) * cap, 1e-30)


def removal_kernel(layout, info_ref, tot_ref, cap_ref, *rest):
    groups, (out_ref, w_ref) = grouped(rest, layout)
    inside = jnp.max(info_ref[:, 2:3]) > 0.0

    @pl.when((pl.program_id(0) == 0) & inside)
    def _():
        chosen = coefficients(tot_ref, out_ref.shape[0])
        widened(chosen / reach(chosen, cap_ref), w_ref)

    @pl.when(inside)
    def _():
        for y in range(0, out_ref.shape[2], TILE):
            out_ref[:, 0, y : y + TILE, :] = combined(w_ref, groups, pl.program_id(0), y)


def removals(info, tot, cap, slots, count):
    flat, layout = laid_out(slots)
    shape = (count,) + tuple(as_piece(slots[0][0])[1][1:])
    return pl.pallas_call(
        functools.partial(removal_kernel, layout),
        grid=(shape[1],),
        in_specs=[whole_spec(info.shape), whole_spec(tot.shape), whole_spec(cap.shape)]
        + [DIRECT] * len(flat),
        out_specs=plane_spec(shape, same_plane),
        out_shape=near(shape, F32),
        scratch_shapes=[
            pltpu.VMEM((2 * count * TILE, len(slots) * layout[0][0][0] * TILE), BF16),
        ],
        compiler_params=params(6),
        cost_estimate=pl.CostEstimate(
            flops=2 * 2 * 256 * 1024 * 384, bytes_accessed=4 * MIB, transcendentals=0
        ),
        name="removals",
    )(info, tot, cap, *flat)


def image_kernel(
    planes, info_ref, low_ref, high_ref, v_ref, wide_in, r_ref, x_ref,
    new_ref, image_ref, curve_ref, keep_ref, n_ref, r_near, x_near, ky, kz, even, odd, total, sem,
):
    i = pl.program_id(0)
    count, _, rows, depth = n_ref.shape

    @pl.when(i == 0)
    def _():
        ky[...] = band_matrix(count * rows, rows)
        kz[...] = band_matrix(depth, depth)
        total[...] = jnp.zeros_like(total)
        pltpu.make_async_copy(r_ref, r_near, sem.at[0]).start()
        pltpu.make_async_copy(x_ref, x_near, sem.at[1]).start()
        n_ref[:, 0:3] = low_ref[...].astype(F32)
        n_ref[:, planes + 3 : planes + 6] = high_ref[...].astype(F32)

    for half, beside in enumerate((even, odd)):
        high, low = split(n_ref[:, 2 * i + half + 3].reshape(count * rows, depth))
        sides = dot(ky[...], high) + dot(ky[...], low) + dot(high, kz[...]) + dot(low, kz[...])
        beside[...] = sides.reshape(beside.shape)
    for half, beside in enumerate((even, odd)):
        plane = 2 * i + half + 3
        shifted = v_ref[half] - 1.5 * K0
        for c in range(count):
            here = n_ref[c, plane]
            side = beside[c]
            for away in range(1, 4):
                side = side + SIDE[away - 1] * (n_ref[c, plane - away] + n_ref[c, plane + away])
            image = SCALE * side + (shifted - info_ref[c : c + 1, 1:2]) * here
            new_ref[c, half] = here
            keep_ref[c, plane - 3] = here
            image_ref[c, plane - 3] = image
            total[c : c + 1] += jnp.sum(here * image, axis=0, keepdims=True)

    @pl.when(i == planes // 2 - 1)
    def _():
        curve_ref[...] = jnp.broadcast_to(jnp.sum(total[...], axis=1, keepdims=True), curve_ref.shape)
        pltpu.make_async_copy(r_ref, r_near, sem.at[0]).wait()
        pltpu.make_async_copy(x_ref, x_near, sem.at[1]).wait()


def images(info, low, wide, high, potential, residual, solution):
    count, _, rows, depth = wide.shape
    planes = potential.shape[0]
    shape = (count, planes, rows, depth)
    return pl.pallas_call(
        functools.partial(image_kernel, planes),
        grid=(planes // 2,),
        in_specs=[
            whole_spec(info.shape), DIRECT, DIRECT,
            pl.BlockSpec((2, rows, depth), lambda i: (i, 0, 0)),
            DIRECT,
        ]
        + [pl.BlockSpec(memory_space=pl.ANY)] * 2,
        out_specs=[
            pl.BlockSpec((count, 2, rows, depth), lambda i: (0, i, 0, 0)), DIRECT, whole_spec((count, 128)),
        ]
        + [DIRECT] * 4,
        out_shape=[
            pltpu.HBM(shape, F32), near(shape, F32), jax.ShapeDtypeStruct((count, 128), F32),
            near(shape, F32), near(wide.shape, F32), near(shape, F32), near(shape, F32),
        ],
        input_output_aliases={4: 4},
        scratch_shapes=[
            pltpu.VMEM((count * rows, count * rows), BF16),
            pltpu.VMEM((depth, depth), BF16),
            pltpu.VMEM((count, rows, depth), F32),
            pltpu.VMEM((count, rows, depth), F32),
            pltpu.VMEM((count, depth), F32),
            pltpu.SemaphoreType.DMA((2,)),
        ],
        compiler_params=params(8),
        cost_estimate=pl.CostEstimate(flops=4 * 10**9, bytes_accessed=24 * MIB, transcendentals=0),
        name="images",
    )(info, held(low), held(high), far(potential), held(wide), far(residual), far(solution))


def finish_kernel(planes, tot_ref, info_ref, curve_ref, n_ref, image_ref, r_ref, x_ref, sol_ref, res_ref, sol, res, sem):
    product, _ = scalars(tot_ref, info_ref)
    size = jnp.broadcast_to(product / curve_ref[:, 0:1], info_ref.shape)[:, 0:1][:, :, None]
    copies = []
    for plane in range(planes):
        sol[:, plane] = x_ref[:, plane] + size * n_ref[:, plane]
        res[:, plane] = r_ref[:, plane] - size * image_ref[:, plane]
        for number, (source, target) in enumerate(((sol, sol_ref), (res, res_ref))):
            copy = pltpu.make_async_copy(source.at[:, plane], target.at[:, plane], sem.at[number, plane])
            copy.start()
            copies.append(copy)
    for copy in copies:
        copy.wait()


def finish(tot, info, curve, new, image, residual, solution):
    shape = new.shape
    return pl.pallas_call(
        functools.partial(finish_kernel, shape[1]),
        in_specs=[DIRECT] * 7,
        out_specs=[pl.BlockSpec(memory_space=pl.ANY)] * 2,
        out_shape=[pltpu.HBM(shape, F32)] * 2,
        scratch_shapes=[pltpu.VMEM(shape, F32)] * 2 + [pltpu.SemaphoreType.DMA((2, shape[1]))],
        compiler_params=params(8),
        name="finish",
    )(tot, info, curve, held(new), held(image), held(residual), held(solution))


def after(value, *others):
    return lax.optimization_barrier((value, *others))[0]


SWAP = [(0, 1), (1, 0), (2, 3), (3, 2)]
INNER = [(1, 2), (2, 1)]
INWARD = [(0, 1), (3, 2)]
OUTWARD = [(1, 0), (2, 3)]


def grid_sum(value):
    size = lax.axis_size("grid")
    away = lambda x, step: lax.ppermute(x, "grid", [(i, i ^ step) for i in range(size)])
    value = value + away(value, 1)
    stride = 2
    while stride < size:
        if 4 * stride <= size:
            near_by, above, across = (away(value, step * stride) for step in (1, 2, 3))
            value = (value + near_by) + (above + across)
            stride *= 4
        else:
            value = value + away(value, stride)
            stride *= 2
    return value


def hop(value, pairs):
    return lax.ppermute(value, "band", pairs)


def on_device(
    residual,
    direction,
    solution,
    old_product,
    orbitals,
    energies,
    potential,
    column_index,
    panel_index,
):
    count = residual.shape[0]
    bands = orbitals.shape[0]
    groups = lax.axis_size("band")
    place = lax.axis_index("band")
    is_end = (place == 0) | (place == groups - 1)
    ends = lax.axis_size("grid") - 1
    upward = [(i, i + 1) for i in range(ends)]
    downward = [(i + 1, i) for i in range(ends)]
    used = groups * bands

    halves = (orbitals[:, 0:3], orbitals[:, 5:8])
    mid = orbitals[:, 3:5]
    edge_pair = [hop(half, SWAP) for half in halves]
    edge_inner = hop(jnp.concatenate(halves, axis=1), INNER)
    sides = lambda x: [piece(x, bands, 0, 0), piece(x, bands, 0, 3)]

    band_ids = lax.iota(jnp.int32, energies.shape[0])
    picked = jnp.where(
        band_ids[None, :] == (column_index // 3)[:, None], energies[None, :], jnp.float32(0.0)
    )
    energy = jnp.sum(picked, axis=1)
    wide_energy = jnp.broadcast_to(energy[:, None], (count, 128))
    start, direction, lhs, give, tot = prepare(residual, direction, potential, wide_energy, mid)
    lhs = held(lhs)
    kinds = ((0, LANE_S), (0, LANE_R))
    places = (same_plane, high_plane)
    tot = correlate([tot], [lhs], kinds, [far(orbitals)], (0,), edge_plane, 6)

    edge_far = [hop(after(half, tot), INNER) for half in edge_pair]
    edge_next = hop(after(edge_inner, tot), OUTWARD)
    got = hop(give, INWARD)
    for pair, inner, where in zip(edge_pair, sides(edge_inner), places):
        tot = correlate([tot], [lhs], kinds, [pair, inner], (1, 2), where, 3)

    edge_last = [hop(after(edge_far[0], tot), OUTWARD), hop(after(edge_far[1], tot, edge_next), OUTWARD)]
    both = jnp.concatenate([mid, after(got, tot, *edge_far)[2 * count :]])
    both = hop(after(both, edge_next), INNER)
    mid_pair, mid_inner, mid_far = piece(got, bands, 2 * count // bands), piece(both, bands, 0), piece(both, bands, 1)
    mids = [mid, mid_pair, mid_inner, mid_far]
    for nearer, farther, where in zip(sides(edge_next), edge_far, places):
        tot = correlate([tot], [lhs], kinds, [nearer, farther], (2, 3), where, 3)
    given = correlate(
        [jnp.zeros((2 * count, 128), F32)], [piece(got, 2 * count, 0)], kinds,
        [mid, mid_inner, mid_far, mid_pair], (1, 2, 3, -100), same_plane, 2, True,
    )
    tot = correlate([tot], [lhs], kinds, mids, (0, 1, 2, 3), mid_plane, 2)
    taken = hop(after(given, tot), OUTWARD)
    tot = correlate([tot], [lhs], kinds, [edge_last[0]], (3,), same_plane, 3)

    lane = lax.iota(jnp.int32, 128)
    group = jnp.where(
        place < groups // 2,
        jnp.stack([place, 1 - place, jnp.int32(2), jnp.int32(3)]),
        jnp.stack([place, 5 - place, jnp.int32(1), jnp.int32(0)]),
    )
    ids = (group[:, None] * bands + lax.iota(jnp.int32, bands)[None, :]).reshape(used)
    cells = float(residual.shape[1] * lax.axis_size("grid") * residual.shape[2] * residual.shape[3])
    member = jnp.where(ids[None, :] // PB == panel_index[:, None], jnp.float32(1.0 / cells), jnp.float32(0.0))
    member = jnp.pad(member, ((0, 0), (0, 128 - used)), constant_values=1.0)
    inside = jnp.where(is_end, 0.0, 1.0)
    info = jnp.where(
        lane[None, :] == 0,
        old_product[:, None],
        jnp.where(lane[None, :] == 1, energy[:, None], inside),
    )
    cap = given * inside + taken
    tot, cap, info, member = lax.optimization_barrier((tot, cap, info, member))
    tot = correlate([tot, taken], [lhs], kinds, [edge_last[1]], (3,), high_plane, 3, False, member)
    tot = grid_sum(tot)

    slots = [
        [[halves[half]], [edge_pair[half]], [inner, nearer], [edge_far[half], edge_last[half]]]
        for half, inner, nearer in zip(range(2), sides(edge_inner), sides(edge_next))
    ]
    other_tot = hop(tot, INWARD)
    wide, low, *scalings = directions((tot, cap), info, start, direction, slots[0], 3, 3)
    from_right = lax.ppermute(low, "grid", downward)
    lost = removals(info, after(other_tot, low), cap, [[mid_pair], [mid], [mid_inner], [mid_far]], count)
    lost = (lost * jnp.float32(TOP)).astype(jnp.float16)
    wide, high = directions(scalings, after(info, lost), start, direction, slots[1], 3, 8, wide)
    from_left = lax.ppermute(high, "grid", upward)
    lost = hop(lost, OUTWARD).astype(F32) * jnp.float32(1.0 / TOP)
    (wide,) = directions(
        scalings, info, start, direction, [[m] for m in mids], 2, 6, wide, lost
    )
    new, image, curve, keep, _, residual, solution = images(
        info, from_left, wide, from_right, potential, residual, solution
    )
    curve = grid_sum(curve)
    new_solution, new_residual = finish(tot, info, curve, keep, image, residual, solution)
    return new_solution, new_residual, new, scalings[1][2, :, 0]


def solution(mesh):
    tiles = P("band", "grid", None, None)
    return jax.shard_map(
        on_device,
        mesh=mesh,
        in_specs=(tiles, tiles, tiles, P("band"), tiles, P(), P("grid", None, None), P("band"), P("band")),
        out_specs=(tiles, tiles, tiles, P("band")),
        check_vma=False,
    )
```
